128 devices in a mesh: col: 16 (over z, x), gz: 8 (over y, core).
Axes of the slice: x: 4, y: 4, z: 4, core: 2. Of those that a mesh axis runs over, the one named last changes fastest.
Arguments:
- photon_flux_entering: float32 [1024, 16384], P('gz', 'col'), may hold values from 0.5 to 2
- thermal_state_prior: float32 [1024, 16384], P('gz', 'col'), may hold values from 0.8 to 1.5
- opacity_coefficient: float32 [1024, 16384], P('gz', 'col'), may hold values from 0.02 to 0.2
- conductance_scaled: float32 [1024, 16384], P('gz', 'col'), may hold values from 3276.8 to 13107.2
- thermal_inertia: float32 [1024, 16384], P('gz', 'col'), may hold values from 1 to 4
- granule_power: float32 [8, 32768, 128], P('gz', 'col'), may hold values from 0.1 to 2
- granule_holder: int32 [8, 32768, 1], P('gz', 'col'), may hold values from 0 to 15; in each aligned block of 2048 rows (0 to 2047, 2048 to 4095, ..., all dimensions but the last counted through in order) at most 512 rows name the same one
- granule_slot: int32 [8, 32768], P('gz', 'col'), may hold values from 0 to 1023
Outputs:
- photon_flux_final: float32 [1024, 16384], P('gz', 'col')
- thermal_state_final: float32 [1024, 16384], P('gz', 'col')
The draws below stay inside these ranges and needn't reach their ends.
Inputs may be any that keep to these rules, and one draw needn't show every extreme that they name: `granule_holder`: within the 2048 records of one device no owner is named more than 512 times.
All inputs are finite; a program needn't handle non-finite values.
Results may differ from the reference program's by a relative error of at most 0.0003.
Values sent between devices are 32-bit elements; how exact they have to be, the bound alone decides.
No kernel may reach another device: no remote copies, remote signals or barrier semaphores. Data moves between devices by JAX's collectives and lax.ppermute only.
A program may use at most 128 MiB of HBM per device.

```python
import math
import jax
import jax.numpy as jnp
import numpy as np
from jax import lax

CZ = 128
RECS = 2048
NEWTON = 2
SEGS = 8
MOST = 512
LAYER_COUNT = 1024
PROFILE_TOTAL = 16384
N_COL = 16
N_GZ = 8


def with_ends(values, stream_key, least, top_value):
    longest = values.shape.index(max(values.shape))
    spots = []
    for shift in (0, 1):
        where = [jax.random.randint(jax.random.fold_in(stream_key, axis), (), 0, length) for axis, length in enumerate(values.shape)]
        where[longest] = (where[longest] + shift) % values.shape[longest]
        spots.append(tuple(where))
    return values.at[spots[0]].set(least).at[spots[1]].set(top_value)


def level_of(rng, shape, pieces, least, high):
    gain, own = 1.0, jax.random.fold_in(rng, 6)
    for dim, shards_of in pieces:
        steps = jnp.exp(jax.random.uniform(jax.random.fold_in(own, dim), (shards_of,), jnp.float32, least / len(pieces), high / len(pieces)))
        gain = gain * jnp.repeat(steps, shape[dim] // shards_of).reshape([-1 if axis == dim else 1 for axis in range(len(shape))])
    return gain


def deal_out(stream_key, own, number, rows, amount, top, limit, slope):
    order = jax.random.permutation(stream_key, amount)
    packed, ordinary = load_shares(amount, rows * top, limit, slope, True), load_shares(amount, rows * top, limit, slope, False)
    places = jnp.arange(amount)

    def named(lengths, turn):
        used = int((lengths > 0).sum())
        fixed = max(1, used // 4)
        shifted = fixed + (places - fixed + turn * (used - fixed)) % max(1, amount - fixed)
        return jnp.zeros((amount,), jnp.int32).at[order[jnp.where(places < fixed, places, shifted)]].set(jnp.asarray(lengths, jnp.int32))

    lengths = jnp.where(number % 4 == 0, named(packed, number // 4), named(ordinary, number - number // 4 - 1))
    mixed = jax.random.permutation(jax.random.fold_in(own, 3), amount)
    giver, sink = mixed[0:amount // 2 * 2:2], mixed[1:amount // 2 * 2:2]
    slack = jnp.minimum(lengths[giver] - 1, limit - lengths[sink]) // 2
    slack = jnp.where((giver == order[0]) | (sink == order[0]) | (lengths[sink] == 0), 0, jnp.maximum(slack, 0))
    shifted = jax.random.randint(jax.random.fold_in(own, 4), (amount // 2,), 0, 1 << 20) % (slack + 1)
    lengths = lengths.at[giver].add(-shifted).at[sink].add(shifted)
    members = jnp.searchsorted(jnp.cumsum(lengths), jnp.arange(rows * top), side="right").astype(jnp.int32)
    table = members.reshape(top, rows).T
    table = table[jax.random.permutation(jax.random.fold_in(own, 1), rows)]
    turn = jax.random.randint(jax.random.fold_in(own, 2), (rows, 1), 0, top)
    return jnp.take_along_axis(table, (jnp.arange(top)[None, :] + turn) % top, axis=1)


def load_shares(number_of, total, bound, skew, full):
    loads = [(1 << 20) // math.isqrt(rank ** skew) + 1 for rank in range(1, number_of + 1)]
    largest = bound if full else min(bound, max(-(-total // number_of), total * loads[0] // sum(loads)))
    least = 1 if total - largest >= number_of - 1 else 0
    holding, surplus = [largest] + [least] * (number_of - 1), total - largest - least * (number_of - 1)
    while surplus > 0:
        candidates = [i for i in range(1, number_of) if holding[i] < largest] or [i for i in range(1, number_of) if holding[i] < bound]
        pool, remaining = sum([loads[i] for i in candidates]), surplus
        for i in candidates:
            more = min(bound - holding[i], max(1, remaining * loads[i] // pool), surplus)
            holding[i] = holding[i] + more
            surplus = surplus - more
    return np.array(holding)


def setup_inputs(seed: int = 0) -> dict:
    key_of = jax.random.split(jax.random.key(seed), 9)
    photon_flux_entering = jnp.clip(0.5 + 1.5 * jax.random.uniform(key_of[0], (LAYER_COUNT, PROFILE_TOTAL), jnp.float32) ** level_of(key_of[0], (LAYER_COUNT, PROFILE_TOTAL), ((0, 8), (1, 16)), -0.2, 0.2), 0.5, 2.0)
    thermal_state_prior = jnp.clip(0.8 + 0.7 * jax.random.uniform(key_of[1], (LAYER_COUNT, PROFILE_TOTAL), jnp.float32) ** level_of(key_of[1], (LAYER_COUNT, PROFILE_TOTAL), ((0, 8), (1, 16)), -0.2, 0.2), 0.8, 1.5)
    opacity_coefficient = jnp.clip(jnp.exp(math.log(0.2) - 2.3025851 * jax.random.uniform(key_of[2], (LAYER_COUNT, PROFILE_TOTAL), jnp.float32) ** level_of(key_of[2], (LAYER_COUNT, PROFILE_TOTAL), ((0, 8), (1, 16)), -0.2, 0.2)), 0.02, 0.2)
    conductance_scaled = jnp.clip(jnp.exp(math.log(13107.2) - 1.3862944 * jax.random.uniform(key_of[3], (LAYER_COUNT, PROFILE_TOTAL), jnp.float32) ** level_of(key_of[3], (LAYER_COUNT, PROFILE_TOTAL), ((0, 8), (1, 16)), -0.2, 0.2)), 3276.8, 13107.2)
    thermal_inertia = jnp.clip(jnp.exp(math.log(4.0) - 1.3862944 * jax.random.uniform(key_of[4], (LAYER_COUNT, PROFILE_TOTAL), jnp.float32) ** level_of(key_of[4], (LAYER_COUNT, PROFILE_TOTAL), ((0, 8), (1, 16)), -0.2, 0.2)), 1.0, 4.0)
    granule_power = jnp.clip(jnp.exp(math.log(2.0) - 2.9957323 * jax.random.uniform(key_of[5], (N_GZ, N_COL * RECS, 128), jnp.float32) ** level_of(key_of[5], (N_GZ, N_COL * RECS, 128), ((0, 8), (1, 16)), -0.2, 0.2)), 0.1, 2.0)
    granule_holder_keys = jax.random.split(jax.random.fold_in(key_of[6], 1), N_GZ * (N_COL * RECS) // RECS)
    granule_holder_turns = jax.random.permutation(jax.random.fold_in(key_of[6], 3), N_GZ * (N_COL * RECS) // RECS)
    granule_holder = jax.vmap(lambda own, number: deal_out(jax.random.fold_in(key_of[6], 2), own, number, RECS, N_COL, 1, MOST, 2))(granule_holder_keys, granule_holder_turns).reshape((N_GZ, N_COL * RECS, 1))
    granule_slot = with_ends(jax.random.randint(key_of[7], (N_GZ, N_COL * RECS), 0, CZ * SEGS), jax.random.fold_in(key_of[7], 1), 0, (CZ * SEGS) - 1).astype(jnp.int32)
    return dict(photon_flux_entering=photon_flux_entering, thermal_state_prior=thermal_state_prior, opacity_coefficient=opacity_coefficient, conductance_scaled=conductance_scaled, thermal_inertia=thermal_inertia, granule_power=granule_power, granule_holder=granule_holder, granule_slot=granule_slot)


radiative_inertia = 2.0

def line_operator(field, conductance_scaled, diff_up):
    below = jnp.concatenate([jnp.zeros_like(field[:1]), field[:-1]], 0)
    above = jnp.concatenate([field[1:], jnp.zeros_like(field[:1])], 0)
    return conductance_scaled * (field - below) + diff_up * (field - above)

def reference(photon_flux_entering, thermal_state_prior, opacity_coefficient, conductance_scaled, thermal_inertia, granule_power, granule_holder, granule_slot):
    height, width = photon_flux_entering.shape
    diff_up = jnp.concatenate([conductance_scaled[1:], jnp.zeros_like(conductance_scaled[:1])], 0)
    levels = (jnp.arange(N_GZ, dtype=jnp.int32)[:, None] * CZ + granule_slot // SEGS).astype(jnp.int32)
    blocks = (granule_holder[..., 0] * SEGS + granule_slot % SEGS).astype(jnp.int32)
    deposited_power = jnp.zeros((height, width // 128, 128), jnp.float32).at[levels, blocks].add(granule_power)
    deposited_power = deposited_power.reshape(height, width)
    subdiagonal_entries = -conductance_scaled.at[0].set(0.0)
    superdiagonal_entries = -diff_up
    photon_flux_final, thermal_state_final = (photon_flux_entering, thermal_state_prior)
    for step in range(NEWTON):
        coupling_weight = 16.0 * opacity_coefficient * thermal_state_final ** 3
        blackbody_output = 4.0 * opacity_coefficient * thermal_state_final ** 4
        flux_mismatch = line_operator(photon_flux_final, conductance_scaled, diff_up) + radiative_inertia * (photon_flux_final - photon_flux_entering) + opacity_coefficient * photon_flux_final - blackbody_output
        thermal_mismatch = thermal_inertia * (thermal_state_final - thermal_state_prior) + blackbody_output - opacity_coefficient * photon_flux_final - deposited_power
        jacobian_divisor = thermal_inertia + coupling_weight
        forcing_vector = -flux_mismatch - coupling_weight * thermal_mismatch / jacobian_divisor
        main_band_entries = conductance_scaled + diff_up + radiative_inertia + opacity_coefficient * thermal_inertia / jacobian_divisor
        thermal_increment = lax.linalg.tridiagonal_solve(subdiagonal_entries.T, main_band_entries.T, superdiagonal_entries.T, forcing_vector.T[:, :, None])[:, :, 0].T
        photon_flux_final = photon_flux_final + thermal_increment
        thermal_state_final = thermal_state_final + (opacity_coefficient * thermal_increment - thermal_mismatch) / jacobian_divisor
    return (photon_flux_final, thermal_state_final)
```

```python
import jax
import jax.numpy as jnp
from jax import lax
from jax.experimental import pallas as pl
from jax.experimental.pallas import tpu as pltpu
from jax.sharding import PartitionSpec as P

NEWTON = 2


radiative_inertia = 2.0


def passed_along(array, axis, by):
    size = lax.axis_size(axis)
    pairs = [(i, i + by) for i in range(size) if 0 <= i + by < size]
    return lax.ppermute(array, axis, pairs)


def padded_2(cells, sides, width):
    for axis, dim in sides:
        count = lax.axis_size(axis)
        ends = count - 1
        head = lax.slice_in_dim(cells, 0, width, axis=dim)
        tail = lax.slice_in_dim(cells, cells.shape[dim] - width, cells.shape[dim], axis=dim)
        cells = jnp.concatenate(
            [
                lax.ppermute(tail, axis, [(i, (i + 1) % count) for i in range(ends)]),
                cells,
                lax.ppermute(head, axis, [((i + 1) % count, i) for i in range(ends)]),
            ],
            axis=dim,
        )
    return cells


def from_below(values, stride):
    filler = jnp.zeros(values.shape[:-2] + (stride,) + values.shape[-1:], values.dtype)
    return jnp.concatenate([filler, values[..., :-stride, :]], -2)


def from_above(values, stride):
    filler = jnp.zeros(values.shape[:-2] + (stride,) + values.shape[-1:], values.dtype)
    return jnp.concatenate([values[..., stride:, :], filler], -2)


def combine_rows(
    lower_ratio,
    upper_ratio,
    scaled_rhs,
    lower_below,
    upper_below,
    rhs_below,
    lower_above,
    upper_above,
    rhs_above,
):
    pivot = 1.0 - lower_ratio * upper_below - upper_ratio * lower_above
    new_rhs = (scaled_rhs - lower_ratio * rhs_below - upper_ratio * rhs_above) / pivot
    return (-lower_ratio * lower_below / pivot, -upper_ratio * upper_above / pivot, new_rhs)


def reduce_block(lower_ratio, upper_ratio, scaled_rhs):
    height = lower_ratio.shape[0]
    stride = 1
    while stride < height:
        lower_ratio, upper_ratio, scaled_rhs = combine_rows(
            lower_ratio,
            upper_ratio,
            scaled_rhs,
            from_below(lower_ratio, stride),
            from_below(upper_ratio, stride),
            from_below(scaled_rhs, stride),
            from_above(lower_ratio, stride),
            from_above(upper_ratio, stride),
            from_above(scaled_rhs, stride),
        )
        stride = stride * 2
    return scaled_rhs


def chain_levels(stacked):
    count = lax.axis_size("gz")
    stride = 1
    while stride < count:
        below = passed_along(stacked, "gz", stride)
        above = passed_along(stacked, "gz", -stride)
        stacked = jnp.stack(
            combine_rows(
                stacked[0],
                stacked[1],
                stacked[2],
                below[0],
                below[1],
                below[2],
                above[0],
                above[1],
                above[2],
            )
        )
        stride = stride * 2
    return stacked[2]


def gather_sources(granule_power, granule_holder, granule_slot, cell_rows):
    heat = granule_power[0]
    owners = granule_holder[0, :, 0]
    cells = granule_slot[0]
    total = jnp.zeros((cell_rows, 128), jnp.float32)
    n_owner = lax.axis_size("col")
    capacity_slots = 4 * heat.shape[0] // n_owner
    member = (owners[:, None] == jnp.arange(n_owner, dtype=jnp.int32)[None, :]).astype(jnp.int32)
    slots = jnp.sum((jnp.cumsum(member, 0) - 1) * member, 1)
    send_heat = jnp.zeros((n_owner, capacity_slots, 128), jnp.float32).at[owners, slots].set(heat)
    send_cell = (
        jnp.zeros((n_owner, capacity_slots), jnp.float32)
        .at[owners, slots]
        .set(cells.astype(jnp.float32))
    )
    got_heat, got_cell = (
        lax.all_to_all(send_heat, "col", split_axis=0, concat_axis=0, tiled=True),
        lax.all_to_all(send_cell, "col", split_axis=0, concat_axis=0, tiled=True),
    )
    return total.at[got_cell.reshape(-1).astype(jnp.int32)].add(got_heat.reshape(-1, 128))


def general_path(
    photon_flux_entering,
    thermal_state_prior,
    opacity_coefficient,
    conductance_scaled,
    thermal_inertia,
    granule_power,
    granule_holder,
    granule_slot,
):
    height, width = photon_flux_entering.shape
    seg_count = width // 128
    deposited_power = gather_sources(
        granule_power, granule_holder, granule_slot, height * seg_count
    ).reshape(height, width)
    edge = passed_along(conductance_scaled[:1], "gz", -1)
    diff_up = jnp.concatenate([conductance_scaled[1:], edge], 0)
    places = lax.broadcasted_iota(jnp.int32, (height, 1), 0)
    has_below = (lax.axis_index("gz") > 0).astype(jnp.float32)
    subdiagonal_entries = -conductance_scaled * jnp.where(places == 0, has_below, 1.0)
    superdiagonal_entries = -diff_up
    photon_flux_final, thermal_state_final = (photon_flux_entering, thermal_state_prior)
    for step in range(NEWTON):
        coupling_weight = 16.0 * opacity_coefficient * thermal_state_final**3
        blackbody_output = 4.0 * opacity_coefficient * thermal_state_final**4
        padded = padded_2(photon_flux_final, (("gz", 0),), 1)
        below, above = (padded[:-2], padded[2:])
        flux_mismatch = (
            conductance_scaled * (photon_flux_final - below)
            + diff_up * (photon_flux_final - above)
            + radiative_inertia * (photon_flux_final - photon_flux_entering)
            + opacity_coefficient * photon_flux_final
            - blackbody_output
        )
        thermal_mismatch = (
            thermal_inertia * (thermal_state_final - thermal_state_prior)
            + blackbody_output
            - opacity_coefficient * photon_flux_final
            - deposited_power
        )
        jacobian_divisor = thermal_inertia + coupling_weight
        forcing_vector = -flux_mismatch - coupling_weight * thermal_mismatch / jacobian_divisor
        main_band_entries = (
            conductance_scaled
            + diff_up
            + radiative_inertia
            + opacity_coefficient * thermal_inertia / jacobian_divisor
        )
        lower_ratio = subdiagonal_entries / main_band_entries
        upper_ratio = superdiagonal_entries / main_band_entries
        closed_lower = jnp.where((places == 0) | (places == height - 1), 0.0, lower_ratio)
        closed_upper = jnp.where(places >= height - 2, 0.0, upper_ratio)
        right_sides = jnp.stack(
            [
                jnp.where(places == height - 1, 0.0, forcing_vector / main_band_entries),
                jnp.where(places == 0, -lower_ratio, 0.0),
                jnp.where(places == height - 2, -upper_ratio, 0.0)
                + jnp.where(places == height - 1, 1.0, 0.0),
            ]
        )
        local = reduce_block(closed_lower, closed_upper, right_sides)
        nearby = passed_along(local[:, 0, :], "gz", -1)
        top_lower = subdiagonal_entries[-1]
        top_upper = superdiagonal_entries[-1]
        alpha = top_lower * local[1, -2]
        beta = main_band_entries[-1] + top_lower * local[2, -2] + top_upper * nearby[1]
        gamma = top_upper * nearby[2]
        value = forcing_vector[-1] - top_lower * local[0, -2] - top_upper * nearby[0]
        stacked = jnp.stack([alpha / beta, gamma / beta, value / beta])
        interface = chain_levels(stacked)
        lower_value = passed_along(interface, "gz", 1)
        thermal_increment = (
            local[0] + local[1] * lower_value[None, :] + local[2] * interface[None, :]
        )
        photon_flux_final = photon_flux_final + thermal_increment
        thermal_state_final = (
            thermal_state_final
            + (opacity_coefficient * thermal_increment - thermal_mismatch) / jacobian_divisor
        )
    return (photon_flux_final, thermal_state_final)


SLOTS = 192
ROOM = 190
F32 = jnp.float32
BF16 = jnp.bfloat16
VMEM = pl.BlockSpec(memory_space=pltpu.VMEM)
SMEM = pl.BlockSpec(memory_space=pltpu.SMEM)


def params(mib):
    return pltpu.CompilerParams(vmem_limit_bytes=mib * 2**20)


def tile(count):
    return jax.ShapeDtypeStruct((count, 8, 128), F32)


def pack_kernel(owner_ref, cell_ref, heat_ref, out_ref, row_vmem, row_smem, sem):
    groups, lanes = owner_ref.shape
    owner, cell = owner_ref[...], cell_ref[...]
    level = lax.shift_right_logical(cell, 3)
    band = lax.shift_right_logical(level, 4)
    target = (level + band + owner) & 15
    place = owner * 64 + band * 8 + (cell & 7) + 1
    place_high = lax.shift_right_logical(place, 5).astype(F32)
    place_low = (place & 31).astype(F32)
    classes = lax.broadcasted_iota(jnp.int32, (16, lanes), 0)
    member = [classes == target[g : g + 1, :] for g in range(groups)]
    member_f = [jnp.where(m, 1.0, 0.0) for m in member]
    source = lax.broadcasted_iota(jnp.int32, (lanes, 2 * lanes), 0)
    sink = lax.broadcasted_iota(jnp.int32, (lanes, 2 * lanes), 1)
    before = jnp.where((source < sink) | (sink >= lanes), 1.0, 0.0).astype(BF16)
    counts = jnp.dot(
        jnp.concatenate(member_f, 0).astype(BF16), before, preferred_element_type=F32
    )
    start = jnp.zeros((16, lanes), F32)
    slots = []
    for g in range(groups):
        ahead = counts[16 * g : 16 * g + 16]
        slots.append(jnp.sum(member_f[g] * (ahead[:, :lanes] + start), 0, keepdims=True))
        start = start + ahead[:, lanes:]
    slot = jnp.concatenate(slots, 0).astype(jnp.int32)
    fits = slot < ROOM
    row_vmem[...] = target * SLOTS + jnp.where(fits, slot, SLOTS - 1)
    copy = pltpu.make_async_copy(row_vmem, row_smem, sem)
    copy.start()
    out_ref[...] = jnp.zeros_like(out_ref)
    named = jnp.where(fits, slot, 4096)
    slot_row = lax.broadcasted_iota(jnp.int32, (2 * lanes, lanes), 0)
    table = jnp.zeros((32, 2 * lanes), F32)
    for g in range(groups):
        weights = jnp.concatenate(
            [member_f[g] * place_high[g : g + 1], member_f[g] * place_low[g : g + 1]], 0
        )
        hits = jnp.where(slot_row == named[g : g + 1], 1.0, 0.0)
        table = table + lax.dot_general(
            weights.astype(BF16),
            hits.astype(BF16),
            (((1,), (1,)), ((), ())),
            preferred_element_type=F32,
        )
    places = table[:16] * 32.0 + table[16:] - 1.0
    over = jnp.max(jnp.where(start > ROOM, 1.0, 0.0))
    lane = lax.broadcasted_iota(jnp.int32, (1, 2 * lanes), 1)
    places = jnp.where(lane == 2 * lanes - 1, over, places)
    copy.wait()

    for g in range(groups):

        @pl.loop(0, lanes, step=16)
        def _(base):
            for i in range(16):
                row = row_smem[g, base + i]
                out_ref[pl.ds(row, 1), :] = heat_ref[pl.ds(g * lanes + base + i, 1), :]

    for m in range(16):
        out_ref[m * SLOTS + ROOM : m * SLOTS + ROOM + 1, :] = places[m : m + 1, :lanes]
        out_ref[m * SLOTS + ROOM + 1 : m * SLOTS + SLOTS, :] = places[m : m + 1, lanes:]


def pack(owner, cell, heat):
    return pl.pallas_call(
        pack_kernel,
        out_shape=jax.ShapeDtypeStruct((16 * SLOTS, 128), F32),
        in_specs=[VMEM, VMEM, VMEM],
        out_specs=VMEM,
        scratch_shapes=[
            pltpu.VMEM((16, 128), jnp.int32),
            pltpu.SMEM((16, 128), jnp.int32),
            pltpu.SemaphoreType.DMA,
        ],
        compiler_params=params(16),
    )(owner, cell, heat)


def sum_kernel(got_ref, out_ref, flag_ref, terms):
    flag = jnp.zeros((1, 128), F32)
    for s in range(16):
        heat = got_ref[s * SLOTS : (s + 1) * SLOTS, :]
        high = heat.astype(BF16)
        terms[s * 256 : s * 256 + SLOTS, :128] = high
        terms[s * 256 : s * 256 + SLOTS, 128:] = (heat - high.astype(F32)).astype(BF16)
        terms[s * 256 + SLOTS : (s + 1) * 256, :] = jnp.zeros((256 - SLOTS, 256), BF16)
        flag = jnp.maximum(flag, got_ref[(s + 1) * SLOTS - 1 : (s + 1) * SLOTS, :])
    lane = lax.broadcasted_iota(jnp.int32, (1, 128), 1)
    flag = jnp.where(lane == 127, flag, 0.0)
    flag_ref[0] = jnp.broadcast_to(flag, (8, 128))

    @pl.loop(0, 8)
    def _(block):
        row = (lax.broadcasted_iota(jnp.int32, (128, 128), 0) + block * 128).astype(F32)
        hits = []
        for s in range(16):
            for part in range(2):
                at = s * SLOTS + ROOM + part
                hits.append(jnp.where(row == got_ref[at : at + 1, :], 1.0, 0.0).astype(BF16))
        both = jnp.dot(jnp.concatenate(hits, 1), terms[...], preferred_element_type=F32)
        out_ref[pl.ds(pl.multiple_of(block * 128, 128), 128), :] = both[:, :128] + both[:, 128:]


def sum_records(got):
    return pl.pallas_call(
        sum_kernel,
        out_shape=(jax.ShapeDtypeStruct((1024, 128), F32), tile(1)),
        in_specs=[VMEM],
        out_specs=(VMEM, VMEM),
        scratch_shapes=[pltpu.VMEM((4096, 256), BF16)],
        compiler_params=params(24),
    )(got)


def row_of(ref, h):
    return ref[pl.ds((h // 8) * 64 + h % 8, 8, stride=8), :]


def prepare_kernel(
    flux_ref, temp_ref, opacity_ref, cond_ref, inertia_ref,
    flux_out, temp_out, opacity_out, inertia_out, face_out,
    loss_out, base_out, share_out, rate_out, gain_out, rest_out, one_out, two_out, port_out,
):
    height = loss_out.shape[0]

    def body(group, carry):
        one, one_flow, two, two_flow = carry
        for sub in range(8):
            h = group * 8 + sub
            at = pl.ds(group * 64 + sub, 8, stride=8)
            flux, temp = flux_ref[at, :], temp_ref[at, :]
            opacity, inertia = opacity_ref[at, :], inertia_ref[at, :]
            face = 1.0 / cond_ref[at, :]
            stiff = 16.0 * opacity * (temp * temp * temp)
            emit = 0.25 * stiff * temp
            rate = 1.0 / (inertia + stiff)
            loss = 2.0 + opacity * inertia * rate
            flux_out[h], temp_out[h] = 2.0 * flux, temp
            opacity_out[h], inertia_out[h] = opacity, inertia
            face_out[h], loss_out[h], rate_out[h] = face, loss, rate
            base_out[h] = 2.0 * flux + emit * inertia * rate
            share_out[h] = stiff * rate
            gain_out[h] = opacity * rate
            rest_out[h] = temp - emit * rate
            one, two = one + face * one_flow, two + face * two_flow
            one_out[h], two_out[h] = one, two
            one_flow, two_flow = one_flow + loss * one, two_flow + loss * two
        return one, one_flow, two, two_flow

    zero = jnp.zeros((8, 128), F32)
    one, one_flow, two, two_flow = lax.fori_loop(
        0, height // 8, body, (zero + 1.0, zero, zero, zero + 1.0)
    )
    port_out[0], port_out[1], port_out[2], port_out[3] = one, two, one_flow, two_flow


def prepare(*fields):
    height = fields[0].shape[0] // 8
    return pl.pallas_call(
        prepare_kernel,
        out_shape=(tile(height),) * 13 + (tile(4),),
        in_specs=[VMEM] * 5,
        out_specs=(VMEM,) * 14,
        compiler_params=params(32),
    )(*fields)


def source_at(where_ref, sums_ref, h):
    band = h // 16
    sender = (h + band + where_ref[0]) & 15
    return sums_ref[sender * 8 + band]


def load_kernel(where_ref, sums_ref, base_ref, share_ref, loss_ref, face_ref, flux_out, port_out):
    height = base_ref.shape[0]

    def body(group, carry):
        value, flow = carry
        for sub in range(8):
            h = group * 8 + sub
            value = value + face_ref[h] * flow
            flux_out[h] = value
            load = base_ref[h] + share_ref[h] * source_at(where_ref, sums_ref, h)
            flow = flow + (loss_ref[h] * value - load)
        return value, flow

    zero = jnp.zeros((8, 128), F32)
    value, flow = lax.fori_loop(0, height // 8, body, (zero, zero))
    port_out[0], port_out[1] = value, flow


def load_blocks(where, sums, base, share, loss, face):
    return pl.pallas_call(
        load_kernel,
        out_shape=(tile(base.shape[0]), tile(2)),
        in_specs=[SMEM] + [VMEM] * 5,
        out_specs=(VMEM, VMEM),
        compiler_params=params(16),
    )(where, sums, base, share, loss, face)


def block_ends(where_ref, port_of):
    me = where_ref[1]
    zero = jnp.zeros((8, 128), F32)
    drop, level = zero, zero
    draw, feed = zero, zero
    for step in range(8):
        low = step
        a, b, c, d, p, j = port_of(me, low)
        scale = 1.0 / (c * drop + d)
        new_drop = (a * drop + b) * scale
        new_level = level * scale + (p - new_drop * j)
        below = low < me
        drop, level = jnp.where(below, new_drop, drop), jnp.where(below, new_level, level)
        high = 7 - step
        a, b, c, d, p, j = port_of(me, high)
        scale = 1.0 / (d + draw * b)
        new_draw = (c + draw * a) * scale
        new_feed = (feed - draw * p - j) * scale
        above = high >= me
        draw, feed = jnp.where(above, new_draw, draw), jnp.where(above, new_feed, feed)
    value = (level + drop * feed) / (1.0 + drop * draw)
    return value, feed - draw * value


def slot_of(me, block):
    apart = me ^ block
    return (apart & 1) * 4 + (apart & 2) + lax.shift_right_logical(apart, 2)


def second_kernel(
    where_ref, matrix_ref, loads_ref, flag_ref, sums_ref, one_ref, two_ref, load_ref, gain_ref, rest_ref,
    rate_ref, flux_ref, temp_ref, opacity_ref, inertia_ref, face_ref,
    one_out, two_out, load_out, gain_out, rest_out, port_out,
):
    height = one_ref.shape[0]

    def port_of(me, block):
        at = slot_of(me, block)
        return tuple(matrix_ref[at * 4 + i] for i in range(4)) + tuple(
            loads_ref[at * 2 + i] for i in range(2)
        )

    value, flow = block_ends(where_ref, port_of)

    def body(group, carry):
        one, one_flow, two, two_flow, load, load_flow = carry
        for sub in range(8):
            h = group * 8 + sub
            source = source_at(where_ref, sums_ref, h)
            light = one_ref[h] * value + two_ref[h] * flow + load_ref[h]
            temp = rest_ref[h] + gain_ref[h] * light + rate_ref[h] * source
            opacity, inertia, face = opacity_ref[h], inertia_ref[h], face_ref[h]
            stiff = 16.0 * opacity * (temp * temp * temp)
            emit = 0.25 * stiff * temp
            rate = 1.0 / (inertia + stiff)
            loss = 2.0 + opacity * inertia * rate
            lag = inertia * (temp - temp_ref[h]) - source
            right = flux_ref[h] + (emit * inertia - stiff * lag) * rate
            gain_out[h] = opacity * rate
            rest_out[h] = temp - (lag + emit) * rate
            one, two, load = one + face * one_flow, two + face * two_flow, load + face * load_flow
            one_out[h], two_out[h], load_out[h] = one, two, load
            one_flow, two_flow = one_flow + loss * one, two_flow + loss * two
            load_flow = load_flow + (loss * load - right)
        return one, one_flow, two, two_flow, load, load_flow

    zero = jnp.zeros((8, 128), F32)
    one, one_flow, two, two_flow, load, load_flow = lax.fori_loop(
        0, height // 8, body, (zero + 1.0, zero, zero, zero + 1.0, zero, zero)
    )
    port_out[0], port_out[1], port_out[2], port_out[3] = one, two, one_flow, two_flow
    port_out[4], port_out[5], port_out[6] = load, load_flow, flag_ref[0]


def second_step(where, *arrays):
    height = arrays[4].shape[0]
    return pl.pallas_call(
        second_kernel,
        out_shape=(tile(height),) * 5 + (tile(7),),
        in_specs=[SMEM] + [VMEM] * len(arrays),
        out_specs=(VMEM,) * 6,
        compiler_params=params(32),
    )(where, *arrays)


def finish_kernel(where_ref, ports_ref, one_ref, two_ref, load_ref, gain_ref, rest_ref, flux_out, temp_out):
    height = one_ref.shape[0]

    def port_of(me, block):
        at = slot_of(me, block)
        return tuple(ports_ref[at * 7 + i] for i in range(6))

    value, flow = block_ends(where_ref, port_of)

    def body(group, carry):
        for sub in range(8):
            h = group * 8 + sub
            at = pl.ds(group * 64 + sub, 8, stride=8)
            light = one_ref[h] * value + two_ref[h] * flow + load_ref[h]
            flux_out[at, :] = light
            temp_out[at, :] = rest_ref[h] + gain_ref[h] * light
        return carry

    lax.fori_loop(0, height // 8, body, 0)


def finish(where, *arrays):
    height = arrays[1].shape[0]
    return pl.pallas_call(
        finish_kernel,
        out_shape=(jax.ShapeDtypeStruct((height * 8, 128), F32),) * 2,
        in_specs=[SMEM] + [VMEM] * len(arrays),
        out_specs=(VMEM, VMEM),
        compiler_params=params(16),
    )(where, *arrays)


def gathered(rows):
    for by in (4, 2, 1):
        rows = jnp.concatenate([rows, lax.ppermute(rows, "gz", [(i, i ^ by) for i in range(8)])], 0)
    return rows


def tiles_of(field):
    height, width = field.shape
    return field.reshape(height // 8, 8, width // 128, 128).transpose(0, 2, 1, 3).reshape(-1, 128)


def field_of(tiles, height, width):
    return tiles.reshape(height // 8, width // 128, 8, 128).transpose(0, 2, 1, 3).reshape(height, width)


def shards(
    photon_flux_entering,
    thermal_state_prior,
    opacity_coefficient,
    conductance_scaled,
    thermal_inertia,
    granule_power,
    granule_holder,
    granule_slot,
):
    height, width = photon_flux_entering.shape
    arguments = (
        photon_flux_entering,
        thermal_state_prior,
        opacity_coefficient,
        conductance_scaled,
        thermal_inertia,
        granule_power,
        granule_holder,
        granule_slot,
    )
    where = jnp.stack([lax.axis_index("col"), lax.axis_index("gz")]).astype(jnp.int32)
    sent = pack(granule_holder.reshape(16, 128), granule_slot.reshape(16, 128), granule_power[0])
    got = lax.all_to_all(sent.reshape(16, SLOTS, 128), "col", 0, 0, tiled=True)
    (
        flux, temp, opacity, inertia, face, loss, base, share, rate, gain, rest, one, two, matrix,
    ) = prepare(*[tiles_of(x) for x in arguments[:5]])
    matrix = gathered(matrix)
    sums, flag = sum_records(got.reshape(16 * SLOTS, 128))
    sums = lax.all_to_all(sums.reshape(16, 64, 128), "col", 0, 0, tiled=True).reshape(128, 8, 128)
    load, loads = load_blocks(where, sums, base, share, loss, face)
    loads = gathered(loads)
    one, two, load, gain, rest, ports = second_step(
        where, matrix, loads, flag, sums, one, two, load, gain, rest, rate, flux, temp, opacity, inertia, face
    )
    ports = gathered(ports)
    crowded = jnp.max(ports.reshape(8, 7, 8, 128)[:, 6, 0, 127]) > 0.5

    def quick(_):
        return tuple(
            field_of(x, height, width) for x in finish(where, ports, one, two, load, gain, rest)
        )

    def general(operands):
        return general_path(*operands)

    return lax.cond(crowded, general, quick, arguments)


def solution(mesh):
    return jax.shard_map(
        shards,
        mesh=mesh,
        in_specs=(
            P("gz", "col"),
            P("gz", "col"),
            P("gz", "col"),
            P("gz", "col"),
            P("gz", "col"),
            P("gz", "col", None),
            P("gz", "col", None),
            P("gz", "col"),
        ),
        out_specs=(P("gz", "col"), P("gz", "col")),
        check_vma=False,
    )
```

```python
import jax
import jax.numpy as jnp
from jax import lax
from jax.experimental import pallas as pl
from jax.experimental.pallas import tpu as pltpu
from jax.sharding import PartitionSpec as P

NEWTON = 2


radiative_inertia = 2.0


def passed_along(array, axis, by):
    size = lax.axis_size(axis)
    pairs = [(i, i + by) for i in range(size) if 0 <= i + by < size]
    return lax.ppermute(array, axis, pairs)


def padded_2(cells, sides, width):
    for axis, dim in sides:
        count = lax.axis_size(axis)
        ends = count - 1
        head = lax.slice_in_dim(cells, 0, width, axis=dim)
        tail = lax.slice_in_dim(cells, cells.shape[dim] - width, cells.shape[dim], axis=dim)
        cells = jnp.concatenate(
            [
                lax.ppermute(tail, axis, [(i, (i + 1) % count) for i in range(ends)]),
                cells,
                lax.ppermute(head, axis, [((i + 1) % count, i) for i in range(ends)]),
            ],
            axis=dim,
        )
    return cells


def from_below(values, stride):
    filler = jnp.zeros(values.shape[:-2] + (stride,) + values.shape[-1:], values.dtype)
    return jnp.concatenate([filler, values[..., :-stride, :]], -2)


def from_above(values, stride):
    filler = jnp.zeros(values.shape[:-2] + (stride,) + values.shape[-1:], values.dtype)
    return jnp.concatenate([values[..., stride:, :], filler], -2)


def combine_rows(
    lower_ratio,
    upper_ratio,
    scaled_rhs,
    lower_below,
    upper_below,
    rhs_below,
    lower_above,
    upper_above,
    rhs_above,
):
    pivot = 1.0 - lower_ratio * upper_below - upper_ratio * lower_above
    new_rhs = (scaled_rhs - lower_ratio * rhs_below - upper_ratio * rhs_above) / pivot
    return (-lower_ratio * lower_below / pivot, -upper_ratio * upper_above / pivot, new_rhs)


def reduce_block(lower_ratio, upper_ratio, scaled_rhs):
    height = lower_ratio.shape[0]
    stride = 1
    while stride < height:
        lower_ratio, upper_ratio, scaled_rhs = combine_rows(
            lower_ratio,
            upper_ratio,
            scaled_rhs,
            from_below(lower_ratio, stride),
            from_below(upper_ratio, stride),
            from_below(scaled_rhs, stride),
            from_above(lower_ratio, stride),
            from_above(upper_ratio, stride),
            from_above(scaled_rhs, stride),
        )
        stride = stride * 2
    return scaled_rhs


def chain_levels(stacked):
    count = lax.axis_size("gz")
    stride = 1
    while stride < count:
        below = passed_along(stacked, "gz", stride)
        above = passed_along(stacked, "gz", -stride)
        stacked = jnp.stack(
            combine_rows(
                stacked[0],
                stacked[1],
                stacked[2],
                below[0],
                below[1],
                below[2],
                above[0],
                above[1],
                above[2],
            )
        )
        stride = stride * 2
    return stacked[2]


def gather_sources(granule_power, granule_holder, granule_slot, cell_rows):
    heat = granule_power[0]
    owners = granule_holder[0, :, 0]
    cells = granule_slot[0]
    total = jnp.zeros((cell_rows, 128), jnp.float32)
    n_owner = lax.axis_size("col")
    capacity_slots = 4 * heat.shape[0] // n_owner
    member = (owners[:, None] == jnp.arange(n_owner, dtype=jnp.int32)[None, :]).astype(jnp.int32)
    slots = jnp.sum((jnp.cumsum(member, 0) - 1) * member, 1)
    send_heat = jnp.zeros((n_owner, capacity_slots, 128), jnp.float32).at[owners, slots].set(heat)
    send_cell = (
        jnp.zeros((n_owner, capacity_slots), jnp.float32)
        .at[owners, slots]
        .set(cells.astype(jnp.float32))
    )
    got_heat, got_cell = (
        lax.all_to_all(send_heat, "col", split_axis=0, concat_axis=0, tiled=True),
        lax.all_to_all(send_cell, "col", split_axis=0, concat_axis=0, tiled=True),
    )
    return total.at[got_cell.reshape(-1).astype(jnp.int32)].add(got_heat.reshape(-1, 128))


def general_path(
    photon_flux_entering,
    thermal_state_prior,
    opacity_coefficient,
    conductance_scaled,
    thermal_inertia,
    granule_power,
    granule_holder,
    granule_slot,
):
    height, width = photon_flux_entering.shape
    seg_count = width // 128
    deposited_power = gather_sources(
        granule_power, granule_holder, granule_slot, height * seg_count
    ).reshape(height, width)
    edge = passed_along(conductance_scaled[:1], "gz", -1)
    diff_up = jnp.concatenate([conductance_scaled[1:], edge], 0)
    places = lax.broadcasted_iota(jnp.int32, (height, 1), 0)
    has_below = (lax.axis_index("gz") > 0).astype(jnp.float32)
    subdiagonal_entries = -conductance_scaled * jnp.where(places == 0, has_below, 1.0)
    superdiagonal_entries = -diff_up
    photon_flux_final, thermal_state_final = (photon_flux_entering, thermal_state_prior)
    for step in range(NEWTON):
        coupling_weight = 16.0 * opacity_coefficient * thermal_state_final**3
        blackbody_output = 4.0 * opacity_coefficient * thermal_state_final**4
        padded = padded_2(photon_flux_final, (("gz", 0),), 1)
        below, above = (padded[:-2], padded[2:])
        flux_mismatch = (
            conductance_scaled * (photon_flux_final - below)
            + diff_up * (photon_flux_final - above)
            + radiative_inertia * (photon_flux_final - photon_flux_entering)
            + opacity_coefficient * photon_flux_final
            - blackbody_output
        )
        thermal_mismatch = (
            thermal_inertia * (thermal_state_final - thermal_state_prior)
            + blackbody_output
            - opacity_coefficient * photon_flux_final
            - deposited_power
        )
        jacobian_divisor = thermal_inertia + coupling_weight
        forcing_vector = -flux_mismatch - coupling_weight * thermal_mismatch / jacobian_divisor
        main_band_entries = (
            conductance_scaled
            + diff_up
            + radiative_inertia
            + opacity_coefficient * thermal_inertia / jacobian_divisor
        )
        lower_ratio = subdiagonal_entries / main_band_entries
        upper_ratio = superdiagonal_entries / main_band_entries
        closed_lower = jnp.where((places == 0) | (places == height - 1), 0.0, lower_ratio)
        closed_upper = jnp.where(places >= height - 2, 0.0, upper_ratio)
        right_sides = jnp.stack(
            [
                jnp.where(places == height - 1, 0.0, forcing_vector / main_band_entries),
                jnp.where(places == 0, -lower_ratio, 0.0),
                jnp.where(places == height - 2, -upper_ratio, 0.0)
                + jnp.where(places == height - 1, 1.0, 0.0),
            ]
        )
        local = reduce_block(closed_lower, closed_upper, right_sides)
        nearby = passed_along(local[:, 0, :], "gz", -1)
        top_lower = subdiagonal_entries[-1]
        top_upper = superdiagonal_entries[-1]
        alpha = top_lower * local[1, -2]
        beta = main_band_entries[-1] + top_lower * local[2, -2] + top_upper * nearby[1]
        gamma = top_upper * nearby[2]
        value = forcing_vector[-1] - top_lower * local[0, -2] - top_upper * nearby[0]
        stacked = jnp.stack([alpha / beta, gamma / beta, value / beta])
        interface = chain_levels(stacked)
        lower_value = passed_along(interface, "gz", 1)
        thermal_increment = (
            local[0] + local[1] * lower_value[None, :] + local[2] * interface[None, :]
        )
        photon_flux_final = photon_flux_final + thermal_increment
        thermal_state_final = (
            thermal_state_final
            + (opacity_coefficient * thermal_increment - thermal_mismatch) / jacobian_divisor
        )
    return (photon_flux_final, thermal_state_final)


SLOTS = 192
ROOM = 190
PIECE = 32
F32 = jnp.float32
BF16 = jnp.bfloat16
VMEM = pl.BlockSpec(memory_space=pltpu.VMEM)
SMEM = pl.BlockSpec(memory_space=pltpu.SMEM)
ANY = pl.BlockSpec(memory_space=pl.ANY)
HBM = pl.BlockSpec(memory_space=pltpu.HBM)


def params(mib):
    return pltpu.CompilerParams(vmem_limit_bytes=mib * 2**20)


def tile(*count):
    return jax.ShapeDtypeStruct(count + (8, 128), F32)


def pieces(source, sink, sems, rows):
    return [
        pltpu.make_async_copy(
            source.at[pl.ds(k * rows, rows)], sink.at[pl.ds(k * rows, rows)], sems.at[k]
        )
        for k in range(source.shape[0] // rows)
    ]


def pack_kernel(owner_ref, cell_ref, heat_hbm, out_ref, heat_ref, row_vmem, row_smem, sem, heat_sem):
    heat_copy = pltpu.make_async_copy(heat_hbm, heat_ref, heat_sem)
    heat_copy.start()
    groups, lanes = owner_ref.shape
    owner, cell = owner_ref[...], cell_ref[...]
    level = lax.shift_right_logical(cell, 3)
    band = lax.shift_right_logical(level, 4)
    target = (level + band + owner) & 15
    place = owner * 64 + band * 8 + (cell & 7) + 1
    place_high = lax.shift_right_logical(place, 5).astype(F32)
    place_low = (place & 31).astype(F32)
    classes = lax.broadcasted_iota(jnp.int32, (16, lanes), 0)
    member = [jnp.where(classes == target[g : g + 1, :], 1.0, 0.0) for g in range(groups)]
    source = lax.broadcasted_iota(jnp.int32, (lanes, 2 * lanes), 0)
    sink = lax.broadcasted_iota(jnp.int32, (lanes, 2 * lanes), 1)
    before = jnp.where((source < sink) | (sink >= lanes), 1.0, 0.0).astype(BF16)
    counts = jnp.dot(jnp.concatenate(member, 0).astype(BF16), before, preferred_element_type=F32)
    start = jnp.zeros((16, lanes), F32)
    slots = []
    for g in range(groups):
        ahead = counts[16 * g : 16 * g + 16]
        slots.append(jnp.sum(member[g] * (ahead[:, :lanes] + start), 0, keepdims=True))
        start = start + ahead[:, lanes:]
    slot = jnp.concatenate(slots, 0).astype(jnp.int32)
    fits = slot < ROOM
    row_vmem[...] = target * SLOTS + jnp.where(fits, slot, SLOTS - 1)
    copy = pltpu.make_async_copy(row_vmem, row_smem, sem)
    copy.start()
    out_ref[...] = jnp.zeros_like(out_ref)
    named = jnp.where(fits, slot, 4096)
    slot_row = lax.broadcasted_iota(jnp.int32, (2 * lanes, lanes), 0)
    weights = jnp.concatenate(
        [
            jnp.concatenate([member[g] * part[g : g + 1] for g in range(groups)], 1)
            for part in (place_high, place_low)
        ],
        0,
    ).astype(BF16)
    hits = jnp.concatenate(
        [jnp.where(slot_row == named[g : g + 1], 1.0, 0.0).astype(BF16) for g in range(groups)], 1
    )
    table = lax.dot_general(weights, hits, (((1,), (1,)), ((), ())), preferred_element_type=F32)
    places = table[:16] * 32.0 + table[16:] - 1.0
    over = jnp.max(jnp.where(start > ROOM, 1.0, 0.0))
    lane = lax.broadcasted_iota(jnp.int32, (1, 2 * lanes), 1)
    places = jnp.where(lane == 2 * lanes - 1, over, places)
    copy.wait()
    heat_copy.wait()

    @pl.loop(0, groups)
    def _(g):
        for i in range(lanes):
            row = row_smem[g, i]
            out_ref[pl.ds(row, 1), :] = heat_ref[pl.ds(g * lanes + i, 1), :]

    for m in range(16):
        out_ref[m * SLOTS + ROOM : m * SLOTS + ROOM + 1, :] = places[m : m + 1, :lanes]
        out_ref[m * SLOTS + ROOM + 1 : m * SLOTS + SLOTS, :] = places[m : m + 1, lanes:]


def pack(owner, cell, heat):
    return pl.pallas_call(
        pack_kernel,
        out_shape=jax.ShapeDtypeStruct((16 * SLOTS, 128), F32),
        in_specs=[VMEM, VMEM, HBM],
        out_specs=VMEM,
        scratch_shapes=[
            pltpu.VMEM((2048, 128), F32),
            pltpu.VMEM((16, 128), jnp.int32),
            pltpu.SMEM((16, 128), jnp.int32),
            pltpu.SemaphoreType.DMA,
            pltpu.SemaphoreType.DMA,
        ],
        compiler_params=params(16),
    )(owner, cell, heat)


def sum_kernel(after_ref, got_ref, out_ref, flag_ref, terms):
    flag = jnp.zeros((1, 128), F32)
    for s in range(16):
        heat = got_ref[s * SLOTS : (s + 1) * SLOTS, :]
        high = heat.astype(BF16)
        terms[s * SLOTS : (s + 1) * SLOTS, :128] = high
        terms[s * SLOTS : (s + 1) * SLOTS, 128:] = (heat - high.astype(F32)).astype(BF16)
        flag = jnp.maximum(flag, got_ref[(s + 1) * SLOTS - 1 : (s + 1) * SLOTS, :])
    lane = lax.broadcasted_iota(jnp.int32, (1, 128), 1)
    flag = jnp.where(lane == 127, flag, 0.0)
    flag_ref[0] = jnp.broadcast_to(flag, (8, 128))
    left = lane < 64
    names = []
    for s in range(0, 16, 2):
        rows = [
            got_ref[at : at + 1, :]
            for block in (s, s + 1)
            for at in (block * SLOTS + ROOM, block * SLOTS + ROOM + 1)
        ]
        turned = pltpu.roll(rows[2], 64, 1)
        names += [
            rows[0],
            jnp.where(left, rows[1], turned),
            jnp.where(left, turned, pltpu.roll(rows[3], 64, 1)),
        ]
    names = jnp.concatenate(names, 1)
    row = lax.broadcasted_iota(jnp.int32, (128, 128), 0).astype(F32).astype(BF16)

    for block in range(8):
        near = (names - block * 128.0).astype(BF16)
        hits = [
            jnp.where(row == near[:, g * 128 : (g + 1) * 128], BF16(1.0), BF16(0.0)) for g in range(24)
        ]
        both = jnp.dot(jnp.concatenate(hits, 1), terms[...], preferred_element_type=F32)
        out_ref[block * 128 : (block + 1) * 128, :] = both[:, :128] + both[:, 128:]


def sum_records(after, got):
    return pl.pallas_call(
        sum_kernel,
        out_shape=(jax.ShapeDtypeStruct((1024, 128), F32), tile(1)),
        in_specs=[ANY, VMEM],
        out_specs=(VMEM, VMEM),
        scratch_shapes=[pltpu.VMEM((16 * SLOTS, 256), BF16)],
        compiler_params=params(24),
    )(after, got)


def first_balance(flux, temp, opacity, inertia):
    stiff = 16.0 * opacity * (temp * temp * temp)
    emit = 0.25 * stiff * temp
    rate = 1.0 / (inertia + stiff)
    loss = 2.0 + opacity * inertia * rate
    return loss, 2.0 * flux + emit * inertia * rate, stiff * rate, emit, rate


def prepare_kernel(
    after_ref, flux_ref, temp_ref, opacity_ref, cond_ref, inertia_ref, weight_out, matrix_out, base_out
):
    height = weight_out.shape[0]

    def body(step, carry):
        value, value_flow, flow, flow_flow, load, load_flow = carry
        for sub in range(8):
            group = height // 8 - 1 - step
            h = group * 8 + 7 - sub
            at = pl.ds(group * 64 + 7 - sub, 8, stride=8)
            loss, base, share, _, _ = first_balance(
                flux_ref[at, :], temp_ref[at, :], opacity_ref[at, :], inertia_ref[at, :]
            )
            face = 1.0 / cond_ref[at, :]
            weight_out[h, 0], weight_out[h, 1] = value_flow * share, flow_flow * share
            load, load_flow = load - value_flow * base, load_flow - flow_flow * base
            value, flow = value + loss * value_flow, flow + loss * flow_flow
            value_flow, flow_flow = value_flow + face * value, flow_flow + face * flow
        return value, value_flow, flow, flow_flow, load, load_flow

    zero = jnp.zeros((8, 128), F32)
    value, value_flow, flow, flow_flow, load, load_flow = lax.fori_loop(
        0, height // 8, body, (zero + 1.0, zero, zero, zero + 1.0, zero, zero)
    )
    matrix_out[0], matrix_out[1], matrix_out[2], matrix_out[3] = value, value_flow, flow, flow_flow
    base_out[0], base_out[1] = load, load_flow


def prepare(after, *fields):
    height = fields[0].shape[0] // 8
    return pl.pallas_call(
        prepare_kernel,
        out_shape=(tile(height, 2), tile(4), tile(2)),
        in_specs=[ANY] + [VMEM] * 5,
        out_specs=(VMEM,) * 3,
        compiler_params=params(16),
    )(after, *fields)


def source_at(where_ref, sums_ref, h):
    band = h // 16
    sender = (h + band + where_ref[0]) & 15
    return sums_ref[sender * 8 + band]


def load_kernel(where_ref, flag_ref, sums_ref, base_ref, weight_ref, port_out):
    height = weight_ref.shape[0]

    def body(group, carry):
        totals = list(carry)
        for sub in range(8):
            h = group * 8 + sub
            source = source_at(where_ref, sums_ref, h)
            for i in range(2):
                at = i * 4 + sub % 4
                totals[at] = totals[at] + weight_ref[h, i] * source
        return tuple(totals)

    zero = jnp.zeros((8, 128), F32)
    totals = lax.fori_loop(0, height // 8, body, (zero,) * 8)
    for i in range(2):
        a, b, c, d = totals[4 * i : 4 * i + 4]
        port_out[i] = base_ref[i] - ((a + b) + (c + d))
    port_out[2] = flag_ref[0]


def load_blocks(where, flag, sums, base, weight):
    return pl.pallas_call(
        load_kernel,
        out_shape=tile(3),
        in_specs=[SMEM] + [VMEM] * 4,
        out_specs=VMEM,
        compiler_params=params(8),
    )(where, flag, sums, base, weight)


def slot_of(me, block):
    steps = (lax.shift_right_logical(block, 1) - lax.shift_right_logical(me, 1)) & 3
    return steps * 2 + ((me ^ block) & 1)


def block_ends(where_ref, port_of):
    me = where_ref[1]
    zero = jnp.zeros((8, 128), F32)
    drop, level = zero, zero
    draw, feed = zero, zero
    for step in range(8):
        low = jnp.int32(step)
        a, b, c, d, p, j = port_of(slot_of(me, low))
        scale = 1.0 / (c * drop + d)
        new_drop = (a * drop + b) * scale
        new_level = level * scale + (p - new_drop * j)
        below = low < me
        drop, level = jnp.where(below, new_drop, drop), jnp.where(below, new_level, level)
        high = jnp.int32(7 - step)
        a, b, c, d, p, j = port_of(slot_of(me, high))
        scale = 1.0 / (d + draw * b)
        new_draw = (c + draw * a) * scale
        new_feed = (feed - draw * p - j) * scale
        above = high >= me
        draw, feed = jnp.where(above, new_draw, draw), jnp.where(above, new_feed, feed)
    value = (level + drop * feed) / (1.0 + drop * draw)
    return value, feed - draw * value


def second_kernel(
    where_ref, matrix_ref, loads_ref, sums_ref, flux_ref, temp_ref, opacity_ref, cond_ref, inertia_ref,
    kept_hbm, port_out, crowded_out, kept_ref, sems,
):
    height = kept_ref.shape[0]

    def port_of(at):
        return tuple(matrix_ref[at * 4 + i] for i in range(4)) + tuple(
            loads_ref[at * 3 + i] for i in range(2)
        )

    light, light_flow = block_ends(where_ref, port_of)
    flag = loads_ref[2]
    for block in range(1, 8):
        flag = jnp.maximum(flag, loads_ref[block * 3 + 2])
    crowded_out[0] = jnp.where(jnp.max(flag) > 0.5, 1, 0)

    def body(group, carry):
        light, light_flow, one, one_flow, two, two_flow, load, load_flow = carry
        for sub in range(8):
            h = group * 8 + sub
            at = pl.ds(group * 64 + sub, 8, stride=8)
            flux, before = flux_ref[at, :], temp_ref[at, :]
            opacity, inertia = opacity_ref[at, :], inertia_ref[at, :]
            face = 1.0 / cond_ref[at, :]
            source = source_at(where_ref, sums_ref, h)
            loss, base, share, emit, rate = first_balance(flux, before, opacity, inertia)
            light = light + face * light_flow
            light_flow = light_flow + (loss * light - (base + share * source))
            temp = before + (opacity * light - emit + source) * rate
            stiff = 16.0 * opacity * (temp * temp * temp)
            emit = 0.25 * stiff * temp
            rate = 1.0 / (inertia + stiff)
            loss = 2.0 + opacity * inertia * rate
            lag = inertia * (temp - before) - source
            right = 2.0 * flux + (emit * inertia - stiff * lag) * rate
            one, two, load = one + face * one_flow, two + face * two_flow, load + face * load_flow
            kept = (one, two, load, opacity * rate, temp - (lag + emit) * rate)
            for i, item in enumerate(kept):
                kept_ref[h, i] = item
            one_flow, two_flow = one_flow + loss * one, two_flow + loss * two
            load_flow = load_flow + (loss * load - right)
        return light, light_flow, one, one_flow, two, two_flow, load, load_flow

    zero = jnp.zeros((8, 128), F32)
    carry = (light, light_flow, zero + 1.0, zero, zero, zero + 1.0, zero, zero)
    leaving = pieces(kept_ref, kept_hbm, sems, PIECE)
    for k, copy in enumerate(leaving):
        carry = lax.fori_loop(k * PIECE // 8, (k + 1) * PIECE // 8, body, carry)
        copy.start()
    _, _, one, one_flow, two, two_flow, load, load_flow = carry
    port_out[0], port_out[1], port_out[2], port_out[3] = one, two, one_flow, two_flow
    port_out[4], port_out[5] = load, load_flow
    for copy in leaving:
        copy.wait()


def second_step(where, matrix, loads, sums, *fields):
    height = fields[0].shape[0] // 8
    return pl.pallas_call(
        second_kernel,
        out_shape=(tile(height, 5), tile(6), jax.ShapeDtypeStruct((1,), jnp.int32)),
        in_specs=[SMEM] + [VMEM] * 8,
        out_specs=(HBM, VMEM, SMEM),
        scratch_shapes=[
            pltpu.VMEM((height, 5, 8, 128), F32),
            pltpu.SemaphoreType.DMA((height // PIECE,)),
        ],
        compiler_params=params(16),
    )(where, matrix, loads, sums, *fields)


def finish_kernel(where_ref, ports_ref, kept_hbm, flux_hbm, temp_hbm, kept_ref, flux_ref, temp_ref, sems):
    height = kept_ref.shape[0]
    copies = pieces(kept_hbm, kept_ref, sems.at[0], PIECE)
    for copy in copies:
        copy.start()

    def port_of(at):
        return tuple(ports_ref[at * 6 + i] for i in range(6))

    value, flow = block_ends(where_ref, port_of)

    def body(group, carry):
        for sub in range(8):
            h = group * 8 + sub
            at = pl.ds(group * 64 + sub, 8, stride=8)
            light = kept_ref[h, 0] * value + kept_ref[h, 1] * flow + kept_ref[h, 2]
            flux_ref[at, :] = light
            temp_ref[at, :] = kept_ref[h, 4] + kept_ref[h, 3] * light
        return carry

    leaving = [
        pieces(flux_ref, flux_hbm, sems.at[1], PIECE * 8),
        pieces(temp_ref, temp_hbm, sems.at[2], PIECE * 8),
    ]
    for k, copy in enumerate(copies):
        copy.wait()
        lax.fori_loop(k * PIECE // 8, (k + 1) * PIECE // 8, body, 0)
        for part in leaving:
            part[k].start()
    for part in leaving:
        for copy in part:
            copy.wait()


def finish(where, ports, kept):
    height = kept.shape[0]
    return pl.pallas_call(
        finish_kernel,
        out_shape=(jax.ShapeDtypeStruct((height * 8, 128), F32),) * 2,
        in_specs=[SMEM, VMEM, HBM],
        out_specs=(HBM, HBM),
        scratch_shapes=[
            pltpu.VMEM((height, 5, 8, 128), F32),
            pltpu.VMEM((height * 8, 128), F32),
            pltpu.VMEM((height * 8, 128), F32),
            pltpu.SemaphoreType.DMA((3, height // PIECE)),
        ],
        compiler_params=params(16),
    )(where, ports, kept)


def gathered(rows):
    rows = jnp.concatenate([rows, lax.ppermute(rows, "gz", [(i, i ^ 1) for i in range(8)])], 0)
    above = [
        lax.ppermute(rows, "gz", [(i, (i - 2 * steps) % 8) for i in range(8)]) for steps in (1, 2, 3)
    ]
    return jnp.concatenate([rows] + above, 0)


def tiles_of(field):
    height, width = field.shape
    return field.reshape(height // 8, 8, width // 128, 128).transpose(0, 2, 1, 3).reshape(-1, 128)


def field_of(tiles, height, width):
    return tiles.reshape(height // 8, width // 128, 8, 128).transpose(0, 2, 1, 3).reshape(height, width)


def shards(
    photon_flux_entering,
    thermal_state_prior,
    opacity_coefficient,
    conductance_scaled,
    thermal_inertia,
    granule_power,
    granule_holder,
    granule_slot,
):
    height, width = photon_flux_entering.shape
    arguments = (
        photon_flux_entering,
        thermal_state_prior,
        opacity_coefficient,
        conductance_scaled,
        thermal_inertia,
        granule_power,
        granule_holder,
        granule_slot,
    )
    where = jnp.stack([lax.axis_index("col"), lax.axis_index("gz")]).astype(jnp.int32)
    sent = pack(granule_holder.reshape(16, 128), granule_slot.reshape(16, 128), granule_power[0])
    got = lax.all_to_all(sent.reshape(16, SLOTS, 128), "col", 0, 0, tiled=True)
    fields = [tiles_of(x) for x in arguments[:5]]
    weight, matrix, base = prepare(sent, *fields)
    matrix = gathered(matrix)
    sums, flag = sum_records(matrix, got.reshape(16 * SLOTS, 128))
    sums = lax.all_to_all(sums.reshape(16, 64, 128), "col", 0, 0, tiled=True).reshape(128, 8, 128)
    loads = gathered(load_blocks(where, flag, sums, base, weight))
    kept, ports, crowded = second_step(where, matrix, loads, sums, *fields)
    ports = gathered(ports)

    def quick(_):
        return tuple(field_of(x, height, width) for x in finish(where, ports, kept))

    def general(operands):
        return general_path(*operands)

    return lax.cond(crowded[0] > 0, general, quick, arguments)


def solution(mesh):
    return jax.shard_map(
        shards,
        mesh=mesh,
        in_specs=(
            P("gz", "col"),
            P("gz", "col"),
            P("gz", "col"),
            P("gz", "col"),
            P("gz", "col"),
            P("gz", "col", None),
            P("gz", "col", None),
            P("gz", "col"),
        ),
        out_specs=(P("gz", "col"), P("gz", "col")),
        check_vma=False,
    )
```

```python
import jax
import jax.numpy as jnp
from jax import lax
from jax.experimental import pallas as pl
from jax.experimental.pallas import tpu as pltpu
from jax.sharding import PartitionSpec as P

NEWTON = 2


radiative_inertia = 2.0


def passed_along(array, axis, by):
    size = lax.axis_size(axis)
    pairs = [(i, i + by) for i in range(size) if 0 <= i + by < size]
    return lax.ppermute(array, axis, pairs)


def padded_2(cells, sides, width):
    for axis, dim in sides:
        count = lax.axis_size(axis)
        ends = count - 1
        head = lax.slice_in_dim(cells, 0, width, axis=dim)
        tail = lax.slice_in_dim(cells, cells.shape[dim] - width, cells.shape[dim], axis=dim)
        cells = jnp.concatenate(
            [
                lax.ppermute(tail, axis, [(i, (i + 1) % count) for i in range(ends)]),
                cells,
                lax.ppermute(head, axis, [((i + 1) % count, i) for i in range(ends)]),
            ],
            axis=dim,
        )
    return cells


def from_below(values, stride):
    filler = jnp.zeros(values.shape[:-2] + (stride,) + values.shape[-1:], values.dtype)
    return jnp.concatenate([filler, values[..., :-stride, :]], -2)


def from_above(values, stride):
    filler = jnp.zeros(values.shape[:-2] + (stride,) + values.shape[-1:], values.dtype)
    return jnp.concatenate([values[..., stride:, :], filler], -2)


def combine_rows(
    lower_ratio,
    upper_ratio,
    scaled_rhs,
    lower_below,
    upper_below,
    rhs_below,
    lower_above,
    upper_above,
    rhs_above,
):
    pivot = 1.0 - lower_ratio * upper_below - upper_ratio * lower_above
    new_rhs = (scaled_rhs - lower_ratio * rhs_below - upper_ratio * rhs_above) / pivot
    return (-lower_ratio * lower_below / pivot, -upper_ratio * upper_above / pivot, new_rhs)


def reduce_block(lower_ratio, upper_ratio, scaled_rhs):
    height = lower_ratio.shape[0]
    stride = 1
    while stride < height:
        lower_ratio, upper_ratio, scaled_rhs = combine_rows(
            lower_ratio,
            upper_ratio,
            scaled_rhs,
            from_below(lower_ratio, stride),
            from_below(upper_ratio, stride),
            from_below(scaled_rhs, stride),
            from_above(lower_ratio, stride),
            from_above(upper_ratio, stride),
            from_above(scaled_rhs, stride),
        )
        stride = stride * 2
    return scaled_rhs


def chain_levels(stacked):
    count = lax.axis_size("gz")
    stride = 1
    while stride < count:
        below = passed_along(stacked, "gz", stride)
        above = passed_along(stacked, "gz", -stride)
        stacked = jnp.stack(
            combine_rows(
                stacked[0],
                stacked[1],
                stacked[2],
                below[0],
                below[1],
                below[2],
                above[0],
                above[1],
                above[2],
            )
        )
        stride = stride * 2
    return stacked[2]


def gather_sources(granule_power, granule_holder, granule_slot, cell_rows):
    heat = granule_power[0]
    owners = granule_holder[0, :, 0]
    cells = granule_slot[0]
    total = jnp.zeros((cell_rows, 128), jnp.float32)
    n_owner = lax.axis_size("col")
    capacity_slots = 4 * heat.shape[0] // n_owner
    member = (owners[:, None] == jnp.arange(n_owner, dtype=jnp.int32)[None, :]).astype(jnp.int32)
    slots = jnp.sum((jnp.cumsum(member, 0) - 1) * member, 1)
    send_heat = jnp.zeros((n_owner, capacity_slots, 128), jnp.float32).at[owners, slots].set(heat)
    send_cell = (
        jnp.zeros((n_owner, capacity_slots), jnp.float32)
        .at[owners, slots]
        .set(cells.astype(jnp.float32))
    )
    got_heat, got_cell = (
        lax.all_to_all(send_heat, "col", split_axis=0, concat_axis=0, tiled=True),
        lax.all_to_all(send_cell, "col", split_axis=0, concat_axis=0, tiled=True),
    )
    return total.at[got_cell.reshape(-1).astype(jnp.int32)].add(got_heat.reshape(-1, 128))


def general_path(
    photon_flux_entering,
    thermal_state_prior,
    opacity_coefficient,
    conductance_scaled,
    thermal_inertia,
    granule_power,
    granule_holder,
    granule_slot,
):
    height, width = photon_flux_entering.shape
    seg_count = width // 128
    deposited_power = gather_sources(
        granule_power, granule_holder, granule_slot, height * seg_count
    ).reshape(height, width)
    edge = passed_along(conductance_scaled[:1], "gz", -1)
    diff_up = jnp.concatenate([conductance_scaled[1:], edge], 0)
    places = lax.broadcasted_iota(jnp.int32, (height, 1), 0)
    has_below = (lax.axis_index("gz") > 0).astype(jnp.float32)
    subdiagonal_entries = -conductance_scaled * jnp.where(places == 0, has_below, 1.0)
    superdiagonal_entries = -diff_up
    photon_flux_final, thermal_state_final = (photon_flux_entering, thermal_state_prior)
    for step in range(NEWTON):
        coupling_weight = 16.0 * opacity_coefficient * thermal_state_final**3
        blackbody_output = 4.0 * opacity_coefficient * thermal_state_final**4
        padded = padded_2(photon_flux_final, (("gz", 0),), 1)
        below, above = (padded[:-2], padded[2:])
        flux_mismatch = (
            conductance_scaled * (photon_flux_final - below)
            + diff_up * (photon_flux_final - above)
            + radiative_inertia * (photon_flux_final - photon_flux_entering)
            + opacity_coefficient * photon_flux_final
            - blackbody_output
        )
        thermal_mismatch = (
            thermal_inertia * (thermal_state_final - thermal_state_prior)
            + blackbody_output
            - opacity_coefficient * photon_flux_final
            - deposited_power
        )
        jacobian_divisor = thermal_inertia + coupling_weight
        forcing_vector = -flux_mismatch - coupling_weight * thermal_mismatch / jacobian_divisor
        main_band_entries = (
            conductance_scaled
            + diff_up
            + radiative_inertia
            + opacity_coefficient * thermal_inertia / jacobian_divisor
        )
        lower_ratio = subdiagonal_entries / main_band_entries
        upper_ratio = superdiagonal_entries / main_band_entries
        closed_lower = jnp.where((places == 0) | (places == height - 1), 0.0, lower_ratio)
        closed_upper = jnp.where(places >= height - 2, 0.0, upper_ratio)
        right_sides = jnp.stack(
            [
                jnp.where(places == height - 1, 0.0, forcing_vector / main_band_entries),
                jnp.where(places == 0, -lower_ratio, 0.0),
                jnp.where(places == height - 2, -upper_ratio, 0.0)
                + jnp.where(places == height - 1, 1.0, 0.0),
            ]
        )
        local = reduce_block(closed_lower, closed_upper, right_sides)
        nearby = passed_along(local[:, 0, :], "gz", -1)
        top_lower = subdiagonal_entries[-1]
        top_upper = superdiagonal_entries[-1]
        alpha = top_lower * local[1, -2]
        beta = main_band_entries[-1] + top_lower * local[2, -2] + top_upper * nearby[1]
        gamma = top_upper * nearby[2]
        value = forcing_vector[-1] - top_lower * local[0, -2] - top_upper * nearby[0]
        stacked = jnp.stack([alpha / beta, gamma / beta, value / beta])
        interface = chain_levels(stacked)
        lower_value = passed_along(interface, "gz", 1)
        thermal_increment = (
            local[0] + local[1] * lower_value[None, :] + local[2] * interface[None, :]
        )
        photon_flux_final = photon_flux_final + thermal_increment
        thermal_state_final = (
            thermal_state_final
            + (opacity_coefficient * thermal_increment - thermal_mismatch) / jacobian_divisor
        )
    return (photon_flux_final, thermal_state_final)


SLOTS = 192
ROOM = 190
PIECE = 32
F32 = jnp.float32
BF16 = jnp.bfloat16
VMEM = pl.BlockSpec(memory_space=pltpu.VMEM)
SMEM = pl.BlockSpec(memory_space=pltpu.SMEM)
ANY = pl.BlockSpec(memory_space=pl.ANY)
HBM = pl.BlockSpec(memory_space=pltpu.HBM)


def params(mib):
    return pltpu.CompilerParams(vmem_limit_bytes=mib * 2**20)


def tile(*count):
    return jax.ShapeDtypeStruct(count + (8, 128), F32)


def pieces(source, sink, sems, rows):
    return [
        pltpu.make_async_copy(
            source.at[pl.ds(k * rows, rows)], sink.at[pl.ds(k * rows, rows)], sems.at[k]
        )
        for k in range(source.shape[0] // rows)
    ]


def pack_kernel(owner_ref, cell_ref, heat_hbm, out_ref, heat_ref, row_vmem, row_smem, sem, heat_sem):
    heat_copy = pltpu.make_async_copy(heat_hbm, heat_ref, heat_sem)
    heat_copy.start()
    groups, lanes = owner_ref.shape
    owner, cell = owner_ref[...], cell_ref[...]
    level = lax.shift_right_logical(cell, 3)
    band = lax.shift_right_logical(level, 4)
    target = (level + band + owner) & 15
    place = owner * 64 + band * 8 + (cell & 7) + 1
    place_high = lax.shift_right_logical(place, 5).astype(F32)
    place_low = (place & 31).astype(F32)
    classes = lax.broadcasted_iota(jnp.int32, (16, lanes), 0)
    member = [jnp.where(classes == target[g : g + 1, :], 1.0, 0.0) for g in range(groups)]
    source = lax.broadcasted_iota(jnp.int32, (lanes, 2 * lanes), 0)
    sink = lax.broadcasted_iota(jnp.int32, (lanes, 2 * lanes), 1)
    before = jnp.where((source < sink) | (sink >= lanes), 1.0, 0.0).astype(BF16)
    counts = jnp.dot(jnp.concatenate(member, 0).astype(BF16), before, preferred_element_type=F32)
    start = jnp.zeros((16, lanes), F32)
    slots = []
    for g in range(groups):
        ahead = counts[16 * g : 16 * g + 16]
        slots.append(jnp.sum(member[g] * (ahead[:, :lanes] + start), 0, keepdims=True))
        start = start + ahead[:, lanes:]
    slot = jnp.concatenate(slots, 0).astype(jnp.int32)
    fits = slot < ROOM
    row_vmem[...] = target * SLOTS + jnp.where(fits, slot, SLOTS - 1)
    copy = pltpu.make_async_copy(row_vmem, row_smem, sem)
    copy.start()
    out_ref[...] = jnp.zeros_like(out_ref)
    named = jnp.where(fits, slot, 4096)
    slot_row = lax.broadcasted_iota(jnp.int32, (2 * lanes, lanes), 0)
    weights = jnp.concatenate(
        [
            jnp.concatenate([member[g] * part[g : g + 1] for g in range(groups)], 1)
            for part in (place_high, place_low)
        ],
        0,
    ).astype(BF16)
    hits = jnp.concatenate(
        [jnp.where(slot_row == named[g : g + 1], 1.0, 0.0).astype(BF16) for g in range(groups)], 1
    )
    table = lax.dot_general(weights, hits, (((1,), (1,)), ((), ())), preferred_element_type=F32)
    places = table[:16] * 32.0 + table[16:] - 1.0
    over = jnp.max(jnp.where(start > ROOM, 1.0, 0.0))
    lane = lax.broadcasted_iota(jnp.int32, (1, 2 * lanes), 1)
    places = jnp.where(lane == 2 * lanes - 1, over, places)
    copy.wait()
    heat_copy.wait()

    @pl.loop(0, groups)
    def _(g):
        for i in range(lanes):
            row = row_smem[g, i]
            out_ref[pl.ds(row, 1), :] = heat_ref[pl.ds(g * lanes + i, 1), :]

    for m in range(16):
        out_ref[m * SLOTS + ROOM : m * SLOTS + ROOM + 1, :] = places[m : m + 1, :lanes]
        out_ref[m * SLOTS + ROOM + 1 : m * SLOTS + SLOTS, :] = places[m : m + 1, lanes:]


def pack(owner, cell, heat):
    return pl.pallas_call(
        pack_kernel,
        out_shape=jax.ShapeDtypeStruct((16 * SLOTS, 128), F32),
        in_specs=[VMEM, VMEM, HBM],
        out_specs=VMEM,
        scratch_shapes=[
            pltpu.VMEM((2048, 128), F32),
            pltpu.VMEM((16, 128), jnp.int32),
            pltpu.SMEM((16, 128), jnp.int32),
            pltpu.SemaphoreType.DMA,
            pltpu.SemaphoreType.DMA,
        ],
        compiler_params=params(16),
    )(owner, cell, heat)


def sum_kernel(after_ref, got_ref, out_ref, flag_ref, terms):
    flag = jnp.zeros((1, 128), F32)
    for s in range(16):
        heat = got_ref[s * SLOTS : (s + 1) * SLOTS, :]
        high = heat.astype(BF16)
        terms[s * SLOTS : (s + 1) * SLOTS, :128] = high
        terms[s * SLOTS : (s + 1) * SLOTS, 128:] = (heat - high.astype(F32)).astype(BF16)
        flag = jnp.maximum(flag, got_ref[(s + 1) * SLOTS - 1 : (s + 1) * SLOTS, :])
    lane = lax.broadcasted_iota(jnp.int32, (1, 128), 1)
    flag = jnp.where(lane == 127, flag, 0.0)
    flag_ref[0] = jnp.broadcast_to(flag, (8, 128))
    left = lane < 64
    names = []
    for s in range(0, 16, 2):
        rows = [
            got_ref[at : at + 1, :]
            for block in (s, s + 1)
            for at in (block * SLOTS + ROOM, block * SLOTS + ROOM + 1)
        ]
        turned = pltpu.roll(rows[2], 64, 1)
        names += [
            rows[0],
            jnp.where(left, rows[1], turned),
            jnp.where(left, turned, pltpu.roll(rows[3], 64, 1)),
        ]
    names = jnp.concatenate(names, 1)
    row = lax.broadcasted_iota(jnp.int32, (128, 128), 0).astype(F32).astype(BF16)

    for block in range(8):
        near = (names - block * 128.0).astype(BF16)
        hits = [
            jnp.where(row == near[:, g * 128 : (g + 1) * 128], BF16(1.0), BF16(0.0)) for g in range(24)
        ]
        both = jnp.dot(jnp.concatenate(hits, 1), terms[...], preferred_element_type=F32)
        out_ref[block * 128 : (block + 1) * 128, :] = both[:, :128] + both[:, 128:]


def sum_records(after, got):
    return pl.pallas_call(
        sum_kernel,
        out_shape=(jax.ShapeDtypeStruct((1024, 128), F32), tile(1)),
        in_specs=[ANY, VMEM],
        out_specs=(VMEM, VMEM),
        scratch_shapes=[pltpu.VMEM((16 * SLOTS, 256), BF16)],
        compiler_params=params(24),
    )(after, got)


def first_balance(flux, temp, opacity, inertia):
    stiff = 16.0 * opacity * (temp * temp * temp)
    emit = 0.25 * stiff * temp
    rate = 1.0 / (inertia + stiff)
    loss = 2.0 + opacity * inertia * rate
    return loss, 2.0 * flux + emit * inertia * rate, stiff * rate, emit, rate


def prepare_kernel(
    after_ref, flux_ref, temp_ref, opacity_ref, cond_ref, inertia_ref, weight_out, matrix_out, base_out
):
    height = weight_out.shape[0]

    def body(step, carry):
        value, value_flow, flow, flow_flow, load, load_flow = carry
        for sub in range(8):
            group = height // 8 - 1 - step
            h = group * 8 + 7 - sub
            at = pl.ds(group * 64 + 7 - sub, 8, stride=8)
            loss, base, share, _, _ = first_balance(
                flux_ref[at, :], temp_ref[at, :], opacity_ref[at, :], inertia_ref[at, :]
            )
            face = 1.0 / cond_ref[at, :]
            weight_out[h, 0], weight_out[h, 1] = value_flow * share, flow_flow * share
            load, load_flow = load - value_flow * base, load_flow - flow_flow * base
            value, flow = value + loss * value_flow, flow + loss * flow_flow
            value_flow, flow_flow = value_flow + face * value, flow_flow + face * flow
        return value, value_flow, flow, flow_flow, load, load_flow

    zero = jnp.zeros((8, 128), F32)
    value, value_flow, flow, flow_flow, load, load_flow = lax.fori_loop(
        0, height // 8, body, (zero + 1.0, zero, zero, zero + 1.0, zero, zero)
    )
    matrix_out[0], matrix_out[1], matrix_out[2], matrix_out[3] = value, value_flow, flow, flow_flow
    base_out[0], base_out[1] = load, load_flow


def prepare(after, *fields):
    height = fields[0].shape[0] // 8
    return pl.pallas_call(
        prepare_kernel,
        out_shape=(tile(height, 2), tile(4), tile(2)),
        in_specs=[ANY] + [VMEM] * 5,
        out_specs=(VMEM,) * 3,
        compiler_params=params(16),
    )(after, *fields)


def source_at(where_ref, sums_ref, h):
    band = h // 16
    sender = (h + band + where_ref[0]) & 15
    return sums_ref[sender * 8 + band]


def load_kernel(where_ref, flag_ref, sums_ref, base_ref, weight_ref, port_out):
    height = weight_ref.shape[0]

    def body(group, carry):
        totals = list(carry)
        for sub in range(8):
            h = group * 8 + sub
            source = source_at(where_ref, sums_ref, h)
            for i in range(2):
                at = i * 4 + sub % 4
                totals[at] = totals[at] + weight_ref[h, i] * source
        return tuple(totals)

    zero = jnp.zeros((8, 128), F32)
    totals = lax.fori_loop(0, height // 8, body, (zero,) * 8)
    for i in range(2):
        a, b, c, d = totals[4 * i : 4 * i + 4]
        port_out[i] = base_ref[i] - ((a + b) + (c + d))
    port_out[2] = flag_ref[0]


def load_blocks(where, flag, sums, base, weight):
    return pl.pallas_call(
        load_kernel,
        out_shape=tile(3),
        in_specs=[SMEM] + [VMEM] * 4,
        out_specs=VMEM,
        compiler_params=params(8),
    )(where, flag, sums, base, weight)


def slot_of(me, block):
    steps = (lax.shift_right_logical(block, 1) - lax.shift_right_logical(me, 1)) & 3
    return steps * 2 + ((me ^ block) & 1)


def block_ends(where_ref, port_of):
    me = where_ref[1]
    zero = jnp.zeros((8, 128), F32)
    drop, level = zero, zero
    draw, feed = zero, zero
    for step in range(8):
        low = jnp.int32(step)
        a, b, c, d, p, j = port_of(slot_of(me, low))
        scale = 1.0 / (c * drop + d)
        new_drop = (a * drop + b) * scale
        new_level = level * scale + (p - new_drop * j)
        below = low < me
        drop, level = jnp.where(below, new_drop, drop), jnp.where(below, new_level, level)
        high = jnp.int32(7 - step)
        a, b, c, d, p, j = port_of(slot_of(me, high))
        scale = 1.0 / (d + draw * b)
        new_draw = (c + draw * a) * scale
        new_feed = (feed - draw * p - j) * scale
        above = high >= me
        draw, feed = jnp.where(above, new_draw, draw), jnp.where(above, new_feed, feed)
    value = (level + drop * feed) / (1.0 + drop * draw)
    return value, feed - draw * value


def middle_kernel(
    after_ref, where_ref, sums_ref, flux_ref, temp_ref, opacity_ref, cond_ref, inertia_ref, kept_out
):
    height = kept_out.shape[0]

    def body(group, carry):
        one, one_flow, two, two_flow, load, load_flow = carry
        for sub in range(8):
            h = group * 8 + sub
            at = pl.ds(group * 64 + sub, 8, stride=8)
            flux, before = flux_ref[at, :], temp_ref[at, :]
            opacity, inertia = opacity_ref[at, :], inertia_ref[at, :]
            face = 1.0 / cond_ref[at, :]
            source = source_at(where_ref, sums_ref, h)
            loss, base, share, emit, rate = first_balance(flux, before, opacity, inertia)
            one, two, load = one + face * one_flow, two + face * two_flow, load + face * load_flow
            kept = (
                one, two, load, face, opacity, inertia, opacity * rate,
                before + (source - emit) * rate, inertia * before + source, 2.0 * flux,
            )
            for i, item in enumerate(kept):
                kept_out[h, i] = item
            one_flow, two_flow = one_flow + loss * one, two_flow + loss * two
            load_flow = load_flow + (loss * load - (base + share * source))
        return one, one_flow, two, two_flow, load, load_flow

    zero = jnp.zeros((8, 128), F32)
    lax.fori_loop(0, height // 8, body, (zero + 1.0, zero, zero, zero + 1.0, zero, zero))


def middle(after, where, sums, *fields):
    height = fields[0].shape[0] // 8
    return pl.pallas_call(
        middle_kernel,
        out_shape=tile(height, 10),
        in_specs=[ANY, SMEM] + [VMEM] * 6,
        out_specs=VMEM,
        compiler_params=params(16),
    )(after, where, sums, *fields)


def second_kernel(where_ref, matrix_ref, loads_ref, middle_ref, kept_out, port_out):
    height = kept_out.shape[0]

    def port_of(at):
        return tuple(matrix_ref[at * 4 + i] for i in range(4)) + tuple(
            loads_ref[at * 3 + i] for i in range(2)
        )

    value, flow = block_ends(where_ref, port_of)

    def body(group, carry):
        one, one_flow, two, two_flow, load, load_flow = carry
        for sub in range(8):
            h = group * 8 + sub
            face, opacity, inertia = middle_ref[h, 3], middle_ref[h, 4], middle_ref[h, 5]
            light = middle_ref[h, 0] * value + middle_ref[h, 1] * flow + middle_ref[h, 2]
            temp = middle_ref[h, 7] + middle_ref[h, 6] * light
            stiff = 16.0 * opacity * (temp * temp * temp)
            emit = 0.25 * stiff * temp
            rate = 1.0 / (inertia + stiff)
            loss = 2.0 + opacity * inertia * rate
            lag = inertia * temp - middle_ref[h, 8]
            right = middle_ref[h, 9] + (emit * inertia - stiff * lag) * rate
            one, two, load = one + face * one_flow, two + face * two_flow, load + face * load_flow
            kept = (one, two, load, opacity * rate, temp - (lag + emit) * rate)
            for i, item in enumerate(kept):
                kept_out[h, i] = item
            one_flow, two_flow = one_flow + loss * one, two_flow + loss * two
            load_flow = load_flow + (loss * load - right)
        return one, one_flow, two, two_flow, load, load_flow

    zero = jnp.zeros((8, 128), F32)
    one, one_flow, two, two_flow, load, load_flow = lax.fori_loop(
        0, height // 8, body, (zero + 1.0, zero, zero, zero + 1.0, zero, zero)
    )
    port_out[0], port_out[1], port_out[2], port_out[3] = one, two, one_flow, two_flow
    port_out[4], port_out[5] = load, load_flow


def second_step(where, matrix, loads, kept):
    height = kept.shape[0]
    return pl.pallas_call(
        second_kernel,
        out_shape=(tile(height, 5), tile(6)),
        in_specs=[SMEM] + [VMEM] * 3,
        out_specs=(VMEM, VMEM),
        compiler_params=params(16),
    )(where, matrix, loads, kept)


def finish_kernel(
    where_ref, loads_ref, ports_ref, kept_ref, flux_hbm, temp_hbm, crowded_out, flux_ref, temp_ref, sems
):
    height = kept_ref.shape[0]
    flag = loads_ref[2]
    for block in range(1, 8):
        flag = jnp.maximum(flag, loads_ref[block * 3 + 2])
    crowded_out[0] = jnp.where(jnp.max(flag) > 0.5, 1, 0)

    def port_of(at):
        return tuple(ports_ref[at * 6 + i] for i in range(6))

    value, flow = block_ends(where_ref, port_of)

    def body(group, carry):
        for sub in range(8):
            h = group * 8 + sub
            at = pl.ds(group * 64 + sub, 8, stride=8)
            light = kept_ref[h, 0] * value + kept_ref[h, 1] * flow + kept_ref[h, 2]
            flux_ref[at, :] = light
            temp_ref[at, :] = kept_ref[h, 4] + kept_ref[h, 3] * light
        return carry

    leaving = [
        pieces(flux_ref, flux_hbm, sems.at[0], PIECE * 8),
        pieces(temp_ref, temp_hbm, sems.at[1], PIECE * 8),
    ]
    for k in range(height // PIECE):
        lax.fori_loop(k * PIECE // 8, (k + 1) * PIECE // 8, body, 0)
        for part in leaving:
            part[k].start()
    for part in leaving:
        for copy in part:
            copy.wait()


def finish(where, loads, ports, kept):
    height = kept.shape[0]
    return pl.pallas_call(
        finish_kernel,
        out_shape=(jax.ShapeDtypeStruct((height * 8, 128), F32),) * 2
        + (jax.ShapeDtypeStruct((1,), jnp.int32),),
        in_specs=[SMEM] + [VMEM] * 3,
        out_specs=(HBM, HBM, SMEM),
        scratch_shapes=[
            pltpu.VMEM((height * 8, 128), F32),
            pltpu.VMEM((height * 8, 128), F32),
            pltpu.SemaphoreType.DMA((2, height // PIECE)),
        ],
        compiler_params=params(16),
    )(where, loads, ports, kept)


def swapped(rows):
    return jnp.concatenate([rows, lax.ppermute(rows, "gz", [(i, i ^ 1) for i in range(8)])], 0)


def spread(rows):
    above = [
        lax.ppermute(rows, "gz", [(i, (i - 2 * steps) % 8) for i in range(8)]) for steps in (1, 2, 3)
    ]
    return jnp.concatenate([rows] + above, 0)


def gathered(rows):
    return spread(swapped(rows))


def tiles_of(field):
    height, width = field.shape
    return field.reshape(height // 8, 8, width // 128, 128).transpose(0, 2, 1, 3).reshape(-1, 128)


def field_of(tiles, height, width):
    return tiles.reshape(height // 8, width // 128, 8, 128).transpose(0, 2, 1, 3).reshape(height, width)


def shards(
    photon_flux_entering,
    thermal_state_prior,
    opacity_coefficient,
    conductance_scaled,
    thermal_inertia,
    granule_power,
    granule_holder,
    granule_slot,
):
    height, width = photon_flux_entering.shape
    arguments = (
        photon_flux_entering,
        thermal_state_prior,
        opacity_coefficient,
        conductance_scaled,
        thermal_inertia,
        granule_power,
        granule_holder,
        granule_slot,
    )
    where = jnp.stack([lax.axis_index("col"), lax.axis_index("gz")]).astype(jnp.int32)
    sent = pack(granule_holder.reshape(16, 128), granule_slot.reshape(16, 128), granule_power[0])
    got = lax.all_to_all(sent.reshape(16, SLOTS, 128), "col", 0, 0, tiled=True)
    fields = [tiles_of(x) for x in arguments[:5]]
    weight, matrix, base = prepare(sent, *fields)
    matrix = gathered(matrix)
    sums, flag = sum_records(matrix, got.reshape(16 * SLOTS, 128))
    sums = lax.all_to_all(sums.reshape(16, 64, 128), "col", 0, 0, tiled=True).reshape(128, 8, 128)
    loads = swapped(load_blocks(where, flag, sums, base, weight))
    cells = middle(loads, where, sums, *fields)
    loads = spread(loads)
    kept, ports = second_step(where, matrix, loads, cells)
    flux, temp, crowded = finish(where, loads, gathered(ports), kept)

    def again(state):
        return general_path(*arguments) + (jnp.zeros_like(state[2]),)

    flux, temp = field_of(flux, height, width), field_of(temp, height, width)
    return lax.while_loop(lambda state: state[2][0] > 0, again, (flux, temp, crowded))[:2]


def solution(mesh):
    return jax.shard_map(
        shards,
        mesh=mesh,
        in_specs=(
            P("gz", "col"),
            P("gz", "col"),
            P("gz", "col"),
            P("gz", "col"),
            P("gz", "col"),
            P("gz", "col", None),
            P("gz", "col", None),
            P("gz", "col"),
        ),
        out_specs=(P("gz", "col"), P("gz", "col")),
        check_vma=False,
    )
```

```python
import jax
import jax.numpy as jnp
from jax import lax
from jax.experimental import pallas as pl
from jax.experimental.pallas import tpu as pltpu
from jax.sharding import PartitionSpec as P

NEWTON = 2


radiative_inertia = 2.0


def passed_along(array, axis, by):
    size = lax.axis_size(axis)
    pairs = [(i, i + by) for i in range(size) if 0 <= i + by < size]
    return lax.ppermute(array, axis, pairs)


def padded_2(cells, sides, width):
    for axis, dim in sides:
        count = lax.axis_size(axis)
        ends = count - 1
        head = lax.slice_in_dim(cells, 0, width, axis=dim)
        tail = lax.slice_in_dim(cells, cells.shape[dim] - width, cells.shape[dim], axis=dim)
        cells = jnp.concatenate(
            [
                lax.ppermute(tail, axis, [(i, (i + 1) % count) for i in range(ends)]),
                cells,
                lax.ppermute(head, axis, [((i + 1) % count, i) for i in range(ends)]),
            ],
            axis=dim,
        )
    return cells


def from_below(values, stride):
    filler = jnp.zeros(values.shape[:-2] + (stride,) + values.shape[-1:], values.dtype)
    return jnp.concatenate([filler, values[..., :-stride, :]], -2)


def from_above(values, stride):
    filler = jnp.zeros(values.shape[:-2] + (stride,) + values.shape[-1:], values.dtype)
    return jnp.concatenate([values[..., stride:, :], filler], -2)


def combine_rows(
    lower_ratio,
    upper_ratio,
    scaled_rhs,
    lower_below,
    upper_below,
    rhs_below,
    lower_above,
    upper_above,
    rhs_above,
):
    pivot = 1.0 - lower_ratio * upper_below - upper_ratio * lower_above
    new_rhs = (scaled_rhs - lower_ratio * rhs_below - upper_ratio * rhs_above) / pivot
    return (-lower_ratio * lower_below / pivot, -upper_ratio * upper_above / pivot, new_rhs)


def reduce_block(lower_ratio, upper_ratio, scaled_rhs):
    height = lower_ratio.shape[0]
    stride = 1
    while stride < height:
        lower_ratio, upper_ratio, scaled_rhs = combine_rows(
            lower_ratio,
            upper_ratio,
            scaled_rhs,
            from_below(lower_ratio, stride),
            from_below(upper_ratio, stride),
            from_below(scaled_rhs, stride),
            from_above(lower_ratio, stride),
            from_above(upper_ratio, stride),
            from_above(scaled_rhs, stride),
        )
        stride = stride * 2
    return scaled_rhs


def chain_levels(stacked):
    count = lax.axis_size("gz")
    stride = 1
    while stride < count:
        below = passed_along(stacked, "gz", stride)
        above = passed_along(stacked, "gz", -stride)
        stacked = jnp.stack(
            combine_rows(
                stacked[0],
                stacked[1],
                stacked[2],
                below[0],
                below[1],
                below[2],
                above[0],
                above[1],
                above[2],
            )
        )
        stride = stride * 2
    return stacked[2]


def gather_sources(granule_power, granule_holder, granule_slot, cell_rows):
    heat = granule_power[0]
    owners = granule_holder[0, :, 0]
    cells = granule_slot[0]
    total = jnp.zeros((cell_rows, 128), jnp.float32)
    n_owner = lax.axis_size("col")
    capacity_slots = 4 * heat.shape[0] // n_owner
    member = (owners[:, None] == jnp.arange(n_owner, dtype=jnp.int32)[None, :]).astype(jnp.int32)
    slots = jnp.sum((jnp.cumsum(member, 0) - 1) * member, 1)
    send_heat = jnp.zeros((n_owner, capacity_slots, 128), jnp.float32).at[owners, slots].set(heat)
    send_cell = (
        jnp.zeros((n_owner, capacity_slots), jnp.float32)
        .at[owners, slots]
        .set(cells.astype(jnp.float32))
    )
    got_heat, got_cell = (
        lax.all_to_all(send_heat, "col", split_axis=0, concat_axis=0, tiled=True),
        lax.all_to_all(send_cell, "col", split_axis=0, concat_axis=0, tiled=True),
    )
    return total.at[got_cell.reshape(-1).astype(jnp.int32)].add(got_heat.reshape(-1, 128))


def general_path(
    photon_flux_entering,
    thermal_state_prior,
    opacity_coefficient,
    conductance_scaled,
    thermal_inertia,
    granule_power,
    granule_holder,
    granule_slot,
):
    height, width = photon_flux_entering.shape
    seg_count = width // 128
    deposited_power = gather_sources(
        granule_power, granule_holder, granule_slot, height * seg_count
    ).reshape(height, width)
    edge = passed_along(conductance_scaled[:1], "gz", -1)
    diff_up = jnp.concatenate([conductance_scaled[1:], edge], 0)
    places = lax.broadcasted_iota(jnp.int32, (height, 1), 0)
    has_below = (lax.axis_index("gz") > 0).astype(jnp.float32)
    subdiagonal_entries = -conductance_scaled * jnp.where(places == 0, has_below, 1.0)
    superdiagonal_entries = -diff_up
    photon_flux_final, thermal_state_final = (photon_flux_entering, thermal_state_prior)
    for step in range(NEWTON):
        coupling_weight = 16.0 * opacity_coefficient * thermal_state_final**3
        blackbody_output = 4.0 * opacity_coefficient * thermal_state_final**4
        padded = padded_2(photon_flux_final, (("gz", 0),), 1)
        below, above = (padded[:-2], padded[2:])
        flux_mismatch = (
            conductance_scaled * (photon_flux_final - below)
            + diff_up * (photon_flux_final - above)
            + radiative_inertia * (photon_flux_final - photon_flux_entering)
            + opacity_coefficient * photon_flux_final
            - blackbody_output
        )
        thermal_mismatch = (
            thermal_inertia * (thermal_state_final - thermal_state_prior)
            + blackbody_output
            - opacity_coefficient * photon_flux_final
            - deposited_power
        )
        jacobian_divisor = thermal_inertia + coupling_weight
        forcing_vector = -flux_mismatch - coupling_weight * thermal_mismatch / jacobian_divisor
        main_band_entries = (
            conductance_scaled
            + diff_up
            + radiative_inertia
            + opacity_coefficient * thermal_inertia / jacobian_divisor
        )
        lower_ratio = subdiagonal_entries / main_band_entries
        upper_ratio = superdiagonal_entries / main_band_entries
        closed_lower = jnp.where((places == 0) | (places == height - 1), 0.0, lower_ratio)
        closed_upper = jnp.where(places >= height - 2, 0.0, upper_ratio)
        right_sides = jnp.stack(
            [
                jnp.where(places == height - 1, 0.0, forcing_vector / main_band_entries),
                jnp.where(places == 0, -lower_ratio, 0.0),
                jnp.where(places == height - 2, -upper_ratio, 0.0)
                + jnp.where(places == height - 1, 1.0, 0.0),
            ]
        )
        local = reduce_block(closed_lower, closed_upper, right_sides)
        nearby = passed_along(local[:, 0, :], "gz", -1)
        top_lower = subdiagonal_entries[-1]
        top_upper = superdiagonal_entries[-1]
        alpha = top_lower * local[1, -2]
        beta = main_band_entries[-1] + top_lower * local[2, -2] + top_upper * nearby[1]
        gamma = top_upper * nearby[2]
        value = forcing_vector[-1] - top_lower * local[0, -2] - top_upper * nearby[0]
        stacked = jnp.stack([alpha / beta, gamma / beta, value / beta])
        interface = chain_levels(stacked)
        lower_value = passed_along(interface, "gz", 1)
        thermal_increment = (
            local[0] + local[1] * lower_value[None, :] + local[2] * interface[None, :]
        )
        photon_flux_final = photon_flux_final + thermal_increment
        thermal_state_final = (
            thermal_state_final
            + (opacity_coefficient * thermal_increment - thermal_mismatch) / jacobian_divisor
        )
    return (photon_flux_final, thermal_state_final)


SLOTS = 192
ROOM = 190
PIECE = 16
F32 = jnp.float32
BF16 = jnp.bfloat16
VMEM = pl.BlockSpec(memory_space=pltpu.VMEM)
SMEM = pl.BlockSpec(memory_space=pltpu.SMEM)
ANY = pl.BlockSpec(memory_space=pl.ANY)
HBM = pl.BlockSpec(memory_space=pltpu.HBM)


def params(mib):
    return pltpu.CompilerParams(vmem_limit_bytes=mib * 2**20)


def tile(*count):
    return jax.ShapeDtypeStruct(count + (8, 128), F32)


def pieces(source, sink, sems, rows):
    return [
        pltpu.make_async_copy(
            source.at[pl.ds(k * rows, rows)], sink.at[pl.ds(k * rows, rows)], sems.at[k]
        )
        for k in range(source.shape[0] // rows)
    ]


def pack_kernel(owner_ref, cell_ref, heat_hbm, out_ref, heat_ref, row_vmem, row_smem, sem, heat_sem):
    heat_copy = pltpu.make_async_copy(heat_hbm, heat_ref, heat_sem)
    heat_copy.start()
    groups, lanes = owner_ref.shape
    owner, cell = owner_ref[...], cell_ref[...]
    level = lax.shift_right_logical(cell, 3)
    band = lax.shift_right_logical(level, 4)
    target = (level + band + owner) & 15
    place = owner * 64 + band * 8 + (cell & 7) + 1
    place_high = lax.shift_right_logical(place, 5).astype(F32)
    place_low = (place & 31).astype(F32)
    classes = lax.broadcasted_iota(jnp.int32, (16, lanes), 0)
    member = [jnp.where(classes == target[g : g + 1, :], 1.0, 0.0) for g in range(groups)]
    source = lax.broadcasted_iota(jnp.int32, (lanes, 2 * lanes), 0)
    sink = lax.broadcasted_iota(jnp.int32, (lanes, 2 * lanes), 1)
    before = jnp.where((source < sink) | (sink >= lanes), 1.0, 0.0).astype(BF16)
    counts = jnp.dot(jnp.concatenate(member, 0).astype(BF16), before, preferred_element_type=F32)
    start = jnp.zeros((16, lanes), F32)
    slots = []
    for g in range(groups):
        ahead = counts[16 * g : 16 * g + 16]
        slots.append(jnp.sum(member[g] * (ahead[:, :lanes] + start), 0, keepdims=True))
        start = start + ahead[:, lanes:]
    slot = jnp.concatenate(slots, 0).astype(jnp.int32)
    fits = slot < ROOM
    row_vmem[...] = target * SLOTS + jnp.where(fits, slot, SLOTS - 1)
    copy = pltpu.make_async_copy(row_vmem, row_smem, sem)
    copy.start()
    out_ref[...] = jnp.zeros_like(out_ref)
    named = jnp.where(fits, slot, 4096)
    slot_row = lax.broadcasted_iota(jnp.int32, (2 * lanes, lanes), 0)
    weights = jnp.concatenate(
        [
            jnp.concatenate([member[g] * part[g : g + 1] for g in range(groups)], 1)
            for part in (place_high, place_low)
        ],
        0,
    ).astype(BF16)
    hits = jnp.concatenate(
        [jnp.where(slot_row == named[g : g + 1], 1.0, 0.0).astype(BF16) for g in range(groups)], 1
    )
    table = lax.dot_general(weights, hits, (((1,), (1,)), ((), ())), preferred_element_type=F32)
    places = table[:16] * 32.0 + table[16:] - 1.0
    over = jnp.max(jnp.where(start > ROOM, 1.0, 0.0))
    lane = lax.broadcasted_iota(jnp.int32, (1, 2 * lanes), 1)
    places = jnp.where(lane == 2 * lanes - 1, over, places)
    copy.wait()
    heat_copy.wait()

    @pl.loop(0, groups)
    def _(g):
        for i in range(lanes):
            row = row_smem[g, i]
            out_ref[pl.ds(row, 1), :] = heat_ref[pl.ds(g * lanes + i, 1), :]

    for m in range(16):
        out_ref[m * SLOTS + ROOM : m * SLOTS + ROOM + 1, :] = places[m : m + 1, :lanes]
        out_ref[m * SLOTS + ROOM + 1 : m * SLOTS + SLOTS, :] = places[m : m + 1, lanes:]


def pack(owner, cell, heat):
    return pl.pallas_call(
        pack_kernel,
        out_shape=jax.ShapeDtypeStruct((16 * SLOTS, 128), F32),
        in_specs=[VMEM, VMEM, HBM],
        out_specs=VMEM,
        scratch_shapes=[
            pltpu.VMEM((2048, 128), F32),
            pltpu.VMEM((16, 128), jnp.int32),
            pltpu.SMEM((16, 128), jnp.int32),
            pltpu.SemaphoreType.DMA,
            pltpu.SemaphoreType.DMA,
        ],
        compiler_params=params(16),
    )(owner, cell, heat)


def sum_kernel(after_ref, got_ref, out_hbm, flag_ref, terms, out_ref, sems):
    flag = jnp.zeros((1, 128), F32)
    for s in range(16):
        heat = got_ref[s * SLOTS : (s + 1) * SLOTS, :]
        high = heat.astype(BF16)
        terms[s * SLOTS : (s + 1) * SLOTS, :128] = high
        terms[s * SLOTS : (s + 1) * SLOTS, 128:] = (heat - high.astype(F32)).astype(BF16)
        flag = jnp.maximum(flag, got_ref[(s + 1) * SLOTS - 1 : (s + 1) * SLOTS, :])
    lane = lax.broadcasted_iota(jnp.int32, (1, 128), 1)
    flag = jnp.where(lane == 127, flag, 0.0)
    flag_ref[0] = jnp.broadcast_to(flag, (8, 128))
    left = lane < 64
    names = []
    for s in range(0, 16, 2):
        rows = [
            got_ref[at : at + 1, :]
            for block in (s, s + 1)
            for at in (block * SLOTS + ROOM, block * SLOTS + ROOM + 1)
        ]
        turned = pltpu.roll(rows[2], 64, 1)
        names += [
            rows[0],
            jnp.where(left, rows[1], turned),
            jnp.where(left, turned, pltpu.roll(rows[3], 64, 1)),
        ]
    names = jnp.concatenate(names, 1)
    row = lax.broadcasted_iota(jnp.int32, (128, 128), 0).astype(F32).astype(BF16)
    leaving = pieces(out_ref, out_hbm, sems, 128)

    for block in range(8):
        near = (names - block * 128.0).astype(BF16)
        hits = [
            jnp.where(row == near[:, g * 128 : (g + 1) * 128], BF16(1.0), BF16(0.0)) for g in range(24)
        ]
        both = jnp.dot(jnp.concatenate(hits, 1), terms[...], preferred_element_type=F32)
        out_ref[block * 128 : (block + 1) * 128, :] = both[:, :128] + both[:, 128:]
        leaving[block].start()
    for copy in leaving:
        copy.wait()


def sum_records(after, got):
    return pl.pallas_call(
        sum_kernel,
        out_shape=(jax.ShapeDtypeStruct((1024, 128), F32), tile(1)),
        in_specs=[ANY, VMEM],
        out_specs=(HBM, VMEM),
        scratch_shapes=[
            pltpu.VMEM((16 * SLOTS, 256), BF16),
            pltpu.VMEM((1024, 128), F32),
            pltpu.SemaphoreType.DMA((8,)),
        ],
        compiler_params=params(24),
    )(after, got)


def first_balance(flux, temp, opacity, inertia):
    stiff = 16.0 * opacity * (temp * temp * temp)
    emit = 0.25 * stiff * temp
    rate = 1.0 / (inertia + stiff)
    loss = 2.0 + opacity * inertia * rate
    return loss, 2.0 * flux + emit * inertia * rate, stiff * rate, emit, rate


def prepare_kernel(
    after_ref, flux_ref, temp_ref, opacity_ref, cond_ref, inertia_ref, weight_out, matrix_out, base_out
):
    height = weight_out.shape[0]

    def body(step, carry):
        value, value_flow, flow, flow_flow, load, load_flow = carry
        for sub in range(8):
            group = height // 8 - 1 - step
            h = group * 8 + 7 - sub
            at = pl.ds(group * 64 + 7 - sub, 8, stride=8)
            loss, base, share, _, _ = first_balance(
                flux_ref[at, :], temp_ref[at, :], opacity_ref[at, :], inertia_ref[at, :]
            )
            face = 1.0 / cond_ref[at, :]
            weight_out[h, 0], weight_out[h, 1] = value_flow * share, flow_flow * share
            load, load_flow = load - value_flow * base, load_flow - flow_flow * base
            value, flow = value + loss * value_flow, flow + loss * flow_flow
            value_flow, flow_flow = value_flow + face * value, flow_flow + face * flow
        return value, value_flow, flow, flow_flow, load, load_flow

    zero = jnp.zeros((8, 128), F32)
    value, value_flow, flow, flow_flow, load, load_flow = lax.fori_loop(
        0, height // 8, body, (zero + 1.0, zero, zero, zero + 1.0, zero, zero)
    )
    matrix_out[0], matrix_out[1], matrix_out[2], matrix_out[3] = value, value_flow, flow, flow_flow
    base_out[0], base_out[1] = load, load_flow


def prepare(after, *fields):
    height = fields[0].shape[0] // 8
    return pl.pallas_call(
        prepare_kernel,
        out_shape=(tile(height, 2), tile(4), tile(2)),
        in_specs=[ANY] + [VMEM] * 5,
        out_specs=(VMEM,) * 3,
        compiler_params=params(16),
    )(after, *fields)


def source_at(where_ref, sums_ref, h):
    band = h // 16
    sender = (h + band + where_ref[0]) & 15
    return sums_ref[sender * 8 + band]


def load_kernel(where_ref, flag_ref, sums_ref, base_ref, weight_ref, port_out):
    height = weight_ref.shape[0]

    def body(group, carry):
        totals = list(carry)
        for sub in range(8):
            h = group * 8 + sub
            source = source_at(where_ref, sums_ref, h)
            for i in range(2):
                at = i * 4 + sub % 4
                totals[at] = totals[at] + weight_ref[h, i] * source
        return tuple(totals)

    zero = jnp.zeros((8, 128), F32)
    totals = (zero,) * 8
    for group in range(height // 8):
        totals = body(group, totals)
    for i in range(2):
        a, b, c, d = totals[4 * i : 4 * i + 4]
        port_out[i] = base_ref[i] - ((a + b) + (c + d))
    port_out[2] = flag_ref[0]


def load_blocks(where, flag, sums, base, weight):
    return pl.pallas_call(
        load_kernel,
        out_shape=tile(3),
        in_specs=[SMEM] + [VMEM] * 4,
        out_specs=VMEM,
        compiler_params=params(8),
    )(where, flag, sums, base, weight)


def slot_of(me, block):
    steps = (lax.shift_right_logical(block, 1) - lax.shift_right_logical(me, 1)) & 3
    other = (me ^ block) & 1
    core = me & 1
    odd = jnp.where(lax.shift_right_logical(steps, 1) == core, 2 + other, 7 - other)
    return jnp.where((steps & 1) == 1, odd, steps * 2 + other)


def block_ends(where_ref, port_of):
    me = where_ref[1]
    zero = jnp.zeros((8, 128), F32)
    drop, level = zero, zero
    draw, feed = zero, zero
    for step in range(8):
        low = jnp.int32(step)
        a, b, c, d, p, j = port_of(slot_of(me, low))
        scale = 1.0 / (c * drop + d)
        new_drop = (a * drop + b) * scale
        new_level = level * scale + (p - new_drop * j)
        below = low < me
        drop, level = jnp.where(below, new_drop, drop), jnp.where(below, new_level, level)
        high = jnp.int32(7 - step)
        a, b, c, d, p, j = port_of(slot_of(me, high))
        scale = 1.0 / (d + draw * b)
        new_draw = (c + draw * a) * scale
        new_feed = (feed - draw * p - j) * scale
        above = high >= me
        draw, feed = jnp.where(above, new_draw, draw), jnp.where(above, new_feed, feed)
    value = (level + drop * feed) / (1.0 + drop * draw)
    return value, feed - draw * value


def middle_kernel(
    after_ref, where_ref, sums_ref, flux_ref, temp_ref, opacity_ref, cond_ref, inertia_ref, kept_out
):
    height = kept_out.shape[0]

    def body(group, carry):
        one, one_flow, two, two_flow, load, load_flow = carry
        for sub in range(8):
            h = group * 8 + sub
            at = pl.ds(group * 64 + sub, 8, stride=8)
            flux, before = flux_ref[at, :], temp_ref[at, :]
            opacity, inertia = opacity_ref[at, :], inertia_ref[at, :]
            face = 1.0 / cond_ref[at, :]
            source = source_at(where_ref, sums_ref, h)
            loss, base, share, emit, rate = first_balance(flux, before, opacity, inertia)
            one, two, load = one + face * one_flow, two + face * two_flow, load + face * load_flow
            kept = (
                one, two, load, face, opacity, inertia, opacity * rate,
                before + (source - emit) * rate, inertia * before + source, 2.0 * flux,
            )
            for i, item in enumerate(kept):
                kept_out[h, i] = item
            one_flow, two_flow = one_flow + loss * one, two_flow + loss * two
            load_flow = load_flow + (loss * load - (base + share * source))
        return one, one_flow, two, two_flow, load, load_flow

    zero = jnp.zeros((8, 128), F32)
    carry = (zero + 1.0, zero, zero, zero + 1.0, zero, zero)
    for group in range(height // 8):
        carry = body(group, carry)


def middle(after, where, sums, *fields):
    height = fields[0].shape[0] // 8
    return pl.pallas_call(
        middle_kernel,
        out_shape=tile(height, 10),
        in_specs=[ANY, SMEM] + [VMEM] * 6,
        out_specs=VMEM,
        compiler_params=params(16),
    )(after, where, sums, *fields)


def second_kernel(where_ref, matrix_ref, loads_ref, middle_ref, kept_out, port_out):
    height = kept_out.shape[0]

    def port_of(at):
        return tuple(matrix_ref[at * 4 + i] for i in range(4)) + tuple(
            loads_ref[at * 3 + i] for i in range(2)
        )

    value, flow = block_ends(where_ref, port_of)

    def body(group, carry):
        one, one_flow, two, two_flow, load, load_flow = carry
        for sub in range(8):
            h = group * 8 + sub
            face, opacity, inertia = middle_ref[h, 3], middle_ref[h, 4], middle_ref[h, 5]
            light = middle_ref[h, 0] * value + middle_ref[h, 1] * flow + middle_ref[h, 2]
            temp = middle_ref[h, 7] + middle_ref[h, 6] * light
            stiff = 16.0 * opacity * (temp * temp * temp)
            emit = 0.25 * stiff * temp
            rate = 1.0 / (inertia + stiff)
            loss = 2.0 + opacity * inertia * rate
            lag = inertia * temp - middle_ref[h, 8]
            right = middle_ref[h, 9] + (emit * inertia - stiff * lag) * rate
            one, two, load = one + face * one_flow, two + face * two_flow, load + face * load_flow
            kept = (one, two, load, opacity * rate, temp - (lag + emit) * rate)
            for i, item in enumerate(kept):
                kept_out[h, i] = item
            one_flow, two_flow = one_flow + loss * one, two_flow + loss * two
            load_flow = load_flow + (loss * load - right)
        return one, one_flow, two, two_flow, load, load_flow

    zero = jnp.zeros((8, 128), F32)
    carry = (zero + 1.0, zero, zero, zero + 1.0, zero, zero)
    for group in range(height // 8):
        carry = body(group, carry)
    one, one_flow, two, two_flow, load, load_flow = carry
    port_out[0], port_out[1], port_out[2], port_out[3] = one, two, one_flow, two_flow
    port_out[4], port_out[5] = load, load_flow


def second_step(where, matrix, loads, kept):
    height = kept.shape[0]
    return pl.pallas_call(
        second_kernel,
        out_shape=(tile(height, 5), tile(6)),
        in_specs=[SMEM] + [VMEM] * 3,
        out_specs=(VMEM, VMEM),
        compiler_params=params(16),
    )(where, matrix, loads, kept)


def finish_kernel(
    where_ref, loads_ref, ports_ref, kept_ref, flux_hbm, temp_hbm, crowded_out, flux_ref, temp_ref, sems
):
    height = kept_ref.shape[0]
    flag = loads_ref[2]
    for block in range(1, 8):
        flag = jnp.maximum(flag, loads_ref[block * 3 + 2])
    crowded_out[0] = jnp.where(jnp.max(flag) > 0.5, 1, 0)

    def port_of(at):
        return tuple(ports_ref[at * 6 + i] for i in range(6))

    value, flow = block_ends(where_ref, port_of)

    def body(group):
        for sub in range(8):
            h = group * 8 + sub
            at = pl.ds(group * 64 + sub, 8, stride=8)
            light = kept_ref[h, 0] * value + kept_ref[h, 1] * flow + kept_ref[h, 2]
            flux_ref[at, :] = light
            temp_ref[at, :] = kept_ref[h, 4] + kept_ref[h, 3] * light

    leaving = [
        pieces(flux_ref, flux_hbm, sems.at[0], PIECE * 8),
        pieces(temp_ref, temp_hbm, sems.at[1], PIECE * 8),
    ]
    for k in range(height // PIECE):
        for group in range(k * PIECE // 8, (k + 1) * PIECE // 8):
            body(group)
        for part in leaving:
            part[k].start()
    for part in leaving:
        for copy in part:
            copy.wait()


def finish(where, loads, ports, kept):
    height = kept.shape[0]
    return pl.pallas_call(
        finish_kernel,
        out_shape=(jax.ShapeDtypeStruct((height * 8, 128), F32),) * 2
        + (jax.ShapeDtypeStruct((1,), jnp.int32),),
        in_specs=[SMEM] + [VMEM] * 3,
        out_specs=(HBM, HBM, SMEM),
        scratch_shapes=[
            pltpu.VMEM((height * 8, 128), F32),
            pltpu.VMEM((height * 8, 128), F32),
            pltpu.SemaphoreType.DMA((2, height // PIECE)),
        ],
        compiler_params=params(16),
    )(where, loads, ports, kept)


def swapped(rows):
    return jnp.concatenate([rows, lax.ppermute(rows, "gz", [(i, i ^ 1) for i in range(8)])], 0)


def spread(rows):
    across = lax.ppermute(rows, "gz", [(i, (i + 4) % 8) for i in range(8)])
    beside = lax.ppermute(rows, "gz", [(i, (i - 2 + 4 * (i % 2)) % 8) for i in range(8)])
    passed = lax.ppermute(beside, "gz", [(i, i ^ 1) for i in range(8)])
    return jnp.concatenate([rows, beside, across, passed], 0)


def gathered(rows):
    return spread(swapped(rows))


def tiles_of(field):
    height, width = field.shape
    return field.reshape(height // 8, 8, width // 128, 128).transpose(0, 2, 1, 3).reshape(-1, 128)


def field_of(tiles, height, width):
    return tiles.reshape(height // 8, width // 128, 8, 128).transpose(0, 2, 1, 3).reshape(height, width)


def shards(
    photon_flux_entering,
    thermal_state_prior,
    opacity_coefficient,
    conductance_scaled,
    thermal_inertia,
    granule_power,
    granule_holder,
    granule_slot,
):
    height, width = photon_flux_entering.shape
    arguments = (
        photon_flux_entering,
        thermal_state_prior,
        opacity_coefficient,
        conductance_scaled,
        thermal_inertia,
        granule_power,
        granule_holder,
        granule_slot,
    )
    where = jnp.stack([lax.axis_index("col"), lax.axis_index("gz")]).astype(jnp.int32)
    sent = pack(granule_holder.reshape(16, 128), granule_slot.reshape(16, 128), granule_power[0])
    got = lax.all_to_all(sent.reshape(16, SLOTS, 128), "col", 0, 0, tiled=True)
    fields = [tiles_of(x) for x in arguments[:5]]
    weight, matrix, base = prepare(sent, *fields)
    matrix = gathered(matrix)
    sums, flag = sum_records(matrix, got.reshape(16 * SLOTS, 128))
    sums = lax.all_to_all(sums.reshape(16, 64, 128), "col", 0, 0, tiled=True).reshape(128, 8, 128)
    loads = swapped(load_blocks(where, flag, sums, base, weight))
    cells = middle(loads, where, sums, *fields)
    loads = spread(loads)
    kept, ports = second_step(where, matrix, loads, cells)
    flux, temp, crowded = finish(where, loads, gathered(ports), kept)

    def again(state):
        return general_path(*arguments) + (jnp.zeros_like(state[2]),)

    flux, temp = field_of(flux, height, width), field_of(temp, height, width)
    return lax.while_loop(lambda state: state[2][0] > 0, again, (flux, temp, crowded))[:2]


def solution(mesh):
    return jax.shard_map(
        shards,
        mesh=mesh,
        in_specs=(
            P("gz", "col"),
            P("gz", "col"),
            P("gz", "col"),
            P("gz", "col"),
            P("gz", "col"),
            P("gz", "col", None),
            P("gz", "col", None),
            P("gz", "col"),
        ),
        out_specs=(P("gz", "col"), P("gz", "col")),
        check_vma=False,
    )
```

```python
import jax
import jax.numpy as jnp
from jax import lax
from jax.experimental import pallas as pl
from jax.experimental.pallas import tpu as pltpu
from jax.sharding import PartitionSpec as P

NEWTON = 2


radiative_inertia = 2.0


def passed_along(array, axis, by):
    size = lax.axis_size(axis)
    pairs = [(i, i + by) for i in range(size) if 0 <= i + by < size]
    return lax.ppermute(array, axis, pairs)


def padded_2(cells, sides, width):
    for axis, dim in sides:
        count = lax.axis_size(axis)
        ends = count - 1
        head = lax.slice_in_dim(cells, 0, width, axis=dim)
        tail = lax.slice_in_dim(cells, cells.shape[dim] - width, cells.shape[dim], axis=dim)
        cells = jnp.concatenate(
            [
                lax.ppermute(tail, axis, [(i, (i + 1) % count) for i in range(ends)]),
                cells,
                lax.ppermute(head, axis, [((i + 1) % count, i) for i in range(ends)]),
            ],
            axis=dim,
        )
    return cells


def from_below(values, stride):
    filler = jnp.zeros(values.shape[:-2] + (stride,) + values.shape[-1:], values.dtype)
    return jnp.concatenate([filler, values[..., :-stride, :]], -2)


def from_above(values, stride):
    filler = jnp.zeros(values.shape[:-2] + (stride,) + values.shape[-1:], values.dtype)
    return jnp.concatenate([values[..., stride:, :], filler], -2)


def combine_rows(
    lower_ratio,
    upper_ratio,
    scaled_rhs,
    lower_below,
    upper_below,
    rhs_below,
    lower_above,
    upper_above,
    rhs_above,
):
    pivot = 1.0 - lower_ratio * upper_below - upper_ratio * lower_above
    new_rhs = (scaled_rhs - lower_ratio * rhs_below - upper_ratio * rhs_above) / pivot
    return (-lower_ratio * lower_below / pivot, -upper_ratio * upper_above / pivot, new_rhs)


def reduce_block(lower_ratio, upper_ratio, scaled_rhs):
    height = lower_ratio.shape[0]
    stride = 1
    while stride < height:
        lower_ratio, upper_ratio, scaled_rhs = combine_rows(
            lower_ratio,
            upper_ratio,
            scaled_rhs,
            from_below(lower_ratio, stride),
            from_below(upper_ratio, stride),
            from_below(scaled_rhs, stride),
            from_above(lower_ratio, stride),
            from_above(upper_ratio, stride),
            from_above(scaled_rhs, stride),
        )
        stride = stride * 2
    return scaled_rhs


def chain_levels(stacked):
    count = lax.axis_size("gz")
    stride = 1
    while stride < count:
        below = passed_along(stacked, "gz", stride)
        above = passed_along(stacked, "gz", -stride)
        stacked = jnp.stack(
            combine_rows(
                stacked[0],
                stacked[1],
                stacked[2],
                below[0],
                below[1],
                below[2],
                above[0],
                above[1],
                above[2],
            )
        )
        stride = stride * 2
    return stacked[2]


def gather_sources(granule_power, granule_holder, granule_slot, cell_rows):
    heat = granule_power[0]
    owners = granule_holder[0, :, 0]
    cells = granule_slot[0]
    total = jnp.zeros((cell_rows, 128), jnp.float32)
    n_owner = lax.axis_size("col")
    capacity_slots = 4 * heat.shape[0] // n_owner
    member = (owners[:, None] == jnp.arange(n_owner, dtype=jnp.int32)[None, :]).astype(jnp.int32)
    slots = jnp.sum((jnp.cumsum(member, 0) - 1) * member, 1)
    send_heat = jnp.zeros((n_owner, capacity_slots, 128), jnp.float32).at[owners, slots].set(heat)
    send_cell = (
        jnp.zeros((n_owner, capacity_slots), jnp.float32)
        .at[owners, slots]
        .set(cells.astype(jnp.float32))
    )
    got_heat, got_cell = (
        lax.all_to_all(send_heat, "col", split_axis=0, concat_axis=0, tiled=True),
        lax.all_to_all(send_cell, "col", split_axis=0, concat_axis=0, tiled=True),
    )
    return total.at[got_cell.reshape(-1).astype(jnp.int32)].add(got_heat.reshape(-1, 128))


def general_path(
    photon_flux_entering,
    thermal_state_prior,
    opacity_coefficient,
    conductance_scaled,
    thermal_inertia,
    granule_power,
    granule_holder,
    granule_slot,
):
    height, width = photon_flux_entering.shape
    seg_count = width // 128
    deposited_power = gather_sources(
        granule_power, granule_holder, granule_slot, height * seg_count
    ).reshape(height, width)
    edge = passed_along(conductance_scaled[:1], "gz", -1)
    diff_up = jnp.concatenate([conductance_scaled[1:], edge], 0)
    places = lax.broadcasted_iota(jnp.int32, (height, 1), 0)
    has_below = (lax.axis_index("gz") > 0).astype(jnp.float32)
    subdiagonal_entries = -conductance_scaled * jnp.where(places == 0, has_below, 1.0)
    superdiagonal_entries = -diff_up
    photon_flux_final, thermal_state_final = (photon_flux_entering, thermal_state_prior)
    for step in range(NEWTON):
        coupling_weight = 16.0 * opacity_coefficient * thermal_state_final**3
        blackbody_output = 4.0 * opacity_coefficient * thermal_state_final**4
        padded = padded_2(photon_flux_final, (("gz", 0),), 1)
        below, above = (padded[:-2], padded[2:])
        flux_mismatch = (
            conductance_scaled * (photon_flux_final - below)
            + diff_up * (photon_flux_final - above)
            + radiative_inertia * (photon_flux_final - photon_flux_entering)
            + opacity_coefficient * photon_flux_final
            - blackbody_output
        )
        thermal_mismatch = (
            thermal_inertia * (thermal_state_final - thermal_state_prior)
            + blackbody_output
            - opacity_coefficient * photon_flux_final
            - deposited_power
        )
        jacobian_divisor = thermal_inertia + coupling_weight
        forcing_vector = -flux_mismatch - coupling_weight * thermal_mismatch / jacobian_divisor
        main_band_entries = (
            conductance_scaled
            + diff_up
            + radiative_inertia
            + opacity_coefficient * thermal_inertia / jacobian_divisor
        )
        lower_ratio = subdiagonal_entries / main_band_entries
        upper_ratio = superdiagonal_entries / main_band_entries
        closed_lower = jnp.where((places == 0) | (places == height - 1), 0.0, lower_ratio)
        closed_upper = jnp.where(places >= height - 2, 0.0, upper_ratio)
        right_sides = jnp.stack(
            [
                jnp.where(places == height - 1, 0.0, forcing_vector / main_band_entries),
                jnp.where(places == 0, -lower_ratio, 0.0),
                jnp.where(places == height - 2, -upper_ratio, 0.0)
                + jnp.where(places == height - 1, 1.0, 0.0),
            ]
        )
        local = reduce_block(closed_lower, closed_upper, right_sides)
        nearby = passed_along(local[:, 0, :], "gz", -1)
        top_lower = subdiagonal_entries[-1]
        top_upper = superdiagonal_entries[-1]
        alpha = top_lower * local[1, -2]
        beta = main_band_entries[-1] + top_lower * local[2, -2] + top_upper * nearby[1]
        gamma = top_upper * nearby[2]
        value = forcing_vector[-1] - top_lower * local[0, -2] - top_upper * nearby[0]
        stacked = jnp.stack([alpha / beta, gamma / beta, value / beta])
        interface = chain_levels(stacked)
        lower_value = passed_along(interface, "gz", 1)
        thermal_increment = (
            local[0] + local[1] * lower_value[None, :] + local[2] * interface[None, :]
        )
        photon_flux_final = photon_flux_final + thermal_increment
        thermal_state_final = (
            thermal_state_final
            + (opacity_coefficient * thermal_increment - thermal_mismatch) / jacobian_divisor
        )
    return (photon_flux_final, thermal_state_final)


SLOTS = 192
ROOM = 190
PIECE = 16
F32 = jnp.float32
BF16 = jnp.bfloat16
VMEM = pl.BlockSpec(memory_space=pltpu.VMEM)
SMEM = pl.BlockSpec(memory_space=pltpu.SMEM)
ANY = pl.BlockSpec(memory_space=pl.ANY)
HBM = pl.BlockSpec(memory_space=pltpu.HBM)


def params(mib):
    return pltpu.CompilerParams(vmem_limit_bytes=mib * 2**20)


def tile(*count):
    return jax.ShapeDtypeStruct(count + (8, 128), F32)


def pieces(source, sink, sems, rows):
    return [
        pltpu.make_async_copy(
            source.at[pl.ds(k * rows, rows)], sink.at[pl.ds(k * rows, rows)], sems.at[k]
        )
        for k in range(source.shape[0] // rows)
    ]


def pack_kernel(owner_ref, cell_ref, heat_hbm, out_ref, heat_ref, row_vmem, row_smem, sem, heat_sem):
    heat_copy = pltpu.make_async_copy(heat_hbm, heat_ref, heat_sem)
    heat_copy.start()
    groups, lanes = owner_ref.shape
    owner, cell = owner_ref[...], cell_ref[...]
    level = lax.shift_right_logical(cell, 3)
    band = lax.shift_right_logical(level, 4)
    target = (level + band + owner) & 15
    place = owner * 64 + band * 8 + (cell & 7) + 1
    place_high = lax.shift_right_logical(place, 5).astype(F32)
    place_low = (place & 31).astype(F32)
    classes = lax.broadcasted_iota(jnp.int32, (16, lanes), 0)
    member = [jnp.where(classes == target[g : g + 1, :], 1.0, 0.0) for g in range(groups)]
    source = lax.broadcasted_iota(jnp.int32, (lanes, 2 * lanes), 0)
    sink = lax.broadcasted_iota(jnp.int32, (lanes, 2 * lanes), 1)
    before = jnp.where((source < sink) | (sink >= lanes), 1.0, 0.0).astype(BF16)
    counts = jnp.dot(jnp.concatenate(member, 0).astype(BF16), before, preferred_element_type=F32)
    start = jnp.zeros((16, lanes), F32)
    slots = []
    for g in range(groups):
        ahead = counts[16 * g : 16 * g + 16]
        slots.append(jnp.sum(member[g] * (ahead[:, :lanes] + start), 0, keepdims=True))
        start = start + ahead[:, lanes:]
    slot = jnp.concatenate(slots, 0).astype(jnp.int32)
    fits = slot < ROOM
    row_vmem[...] = target * SLOTS + jnp.where(fits, slot, SLOTS - 1)
    copy = pltpu.make_async_copy(row_vmem, row_smem, sem)
    copy.start()
    out_ref[...] = jnp.zeros_like(out_ref)
    named = jnp.where(fits, slot, 4096)
    slot_row = lax.broadcasted_iota(jnp.int32, (2 * lanes, lanes), 0)
    weights = jnp.concatenate(
        [
            jnp.concatenate([member[g] * part[g : g + 1] for g in range(groups)], 1)
            for part in (place_high, place_low)
        ],
        0,
    ).astype(BF16)
    hits = jnp.concatenate(
        [jnp.where(slot_row == named[g : g + 1], 1.0, 0.0).astype(BF16) for g in range(groups)], 1
    )
    table = lax.dot_general(weights, hits, (((1,), (1,)), ((), ())), preferred_element_type=F32)
    places = table[:16] * 32.0 + table[16:] - 1.0
    over = jnp.max(jnp.where(start > ROOM, 1.0, 0.0))
    lane = lax.broadcasted_iota(jnp.int32, (1, 2 * lanes), 1)
    places = jnp.where(lane == 2 * lanes - 1, over, places)
    copy.wait()
    heat_copy.wait()

    for g in range(groups):
        for i in range(lanes):
            row = row_smem[g, i]
            out_ref[pl.ds(row, 1), :] = heat_ref[g * lanes + i : g * lanes + i + 1, :]

    for m in range(16):
        out_ref[m * SLOTS + ROOM : m * SLOTS + ROOM + 1, :] = places[m : m + 1, :lanes]
        out_ref[m * SLOTS + ROOM + 1 : m * SLOTS + SLOTS, :] = places[m : m + 1, lanes:]


def pack(owner, cell, heat):
    return pl.pallas_call(
        pack_kernel,
        out_shape=jax.ShapeDtypeStruct((16 * SLOTS, 128), F32),
        in_specs=[VMEM, VMEM, HBM],
        out_specs=VMEM,
        scratch_shapes=[
            pltpu.VMEM((2048, 128), F32),
            pltpu.VMEM((16, 128), jnp.int32),
            pltpu.SMEM((16, 128), jnp.int32),
            pltpu.SemaphoreType.DMA,
            pltpu.SemaphoreType.DMA,
        ],
        compiler_params=params(16),
    )(owner, cell, heat)


def sum_kernel(after_ref, got_ref, out_hbm, flag_ref, terms, out_ref, sems):
    flag = jnp.zeros((1, 128), F32)
    for s in range(16):
        heat = got_ref[s * SLOTS : (s + 1) * SLOTS, :]
        high = heat.astype(BF16)
        terms[s * SLOTS : (s + 1) * SLOTS, :128] = high
        terms[s * SLOTS : (s + 1) * SLOTS, 128:] = (heat - high.astype(F32)).astype(BF16)
        flag = jnp.maximum(flag, got_ref[(s + 1) * SLOTS - 1 : (s + 1) * SLOTS, :])
    lane = lax.broadcasted_iota(jnp.int32, (1, 128), 1)
    flag = jnp.where(lane == 127, flag, 0.0)
    flag_ref[0] = jnp.broadcast_to(flag, (8, 128))
    left = lane < 64
    names = []
    for s in range(0, 16, 2):
        rows = [
            got_ref[at : at + 1, :]
            for block in (s, s + 1)
            for at in (block * SLOTS + ROOM, block * SLOTS + ROOM + 1)
        ]
        turned = pltpu.roll(rows[2], 64, 1)
        names += [
            rows[0],
            jnp.where(left, rows[1], turned),
            jnp.where(left, turned, pltpu.roll(rows[3], 64, 1)),
        ]
    names = jnp.concatenate(names, 1)
    row = lax.broadcasted_iota(jnp.int32, (128, 128), 0).astype(F32).astype(BF16)
    leaving = pieces(out_ref, out_hbm, sems, 128)

    for block in range(8):
        near = (names - block * 128.0).astype(BF16)
        hits = [
            jnp.where(row == near[:, g * 128 : (g + 1) * 128], BF16(1.0), BF16(0.0)) for g in range(24)
        ]
        both = jnp.dot(jnp.concatenate(hits, 1), terms[...], preferred_element_type=F32)
        out_ref[block * 128 : (block + 1) * 128, :] = both[:, :128] + both[:, 128:]
        leaving[block].start()
    for copy in leaving:
        copy.wait()


def sum_records(after, got):
    return pl.pallas_call(
        sum_kernel,
        out_shape=(jax.ShapeDtypeStruct((1024, 128), F32), tile(1)),
        in_specs=[ANY, VMEM],
        out_specs=(HBM, VMEM),
        scratch_shapes=[
            pltpu.VMEM((16 * SLOTS, 256), BF16),
            pltpu.VMEM((1024, 128), F32),
            pltpu.SemaphoreType.DMA((8,)),
        ],
        compiler_params=params(24),
    )(after, got)


def first_balance(flux, temp, opacity, inertia):
    stiff = 16.0 * opacity * (temp * temp * temp)
    emit = 0.25 * stiff * temp
    rate = 1.0 / (inertia + stiff)
    loss = 2.0 + opacity * inertia * rate
    return loss, 2.0 * flux + emit * inertia * rate, stiff * rate, emit, rate


def prepare_kernel(
    after_ref, flux_ref, temp_ref, opacity_ref, cond_ref, inertia_ref, weight_out, matrix_out, base_out
):
    height = weight_out.shape[0]

    def body(step, carry):
        value, value_flow, flow, flow_flow, load, load_flow = carry
        for sub in range(8):
            group = height // 8 - 1 - step
            h = group * 8 + 7 - sub
            at = pl.ds(group * 64 + 7 - sub, 8, stride=8)
            loss, base, share, _, _ = first_balance(
                flux_ref[at, :], temp_ref[at, :], opacity_ref[at, :], inertia_ref[at, :]
            )
            face = 1.0 / cond_ref[at, :]
            weight_out[h, 0], weight_out[h, 1] = value_flow * share, flow_flow * share
            load, load_flow = load - value_flow * base, load_flow - flow_flow * base
            value, flow = value + loss * value_flow, flow + loss * flow_flow
            value_flow, flow_flow = value_flow + face * value, flow_flow + face * flow
        return value, value_flow, flow, flow_flow, load, load_flow

    zero = jnp.zeros((8, 128), F32)
    value, value_flow, flow, flow_flow, load, load_flow = lax.fori_loop(
        0, height // 8, body, (zero + 1.0, zero, zero, zero + 1.0, zero, zero)
    )
    matrix_out[0], matrix_out[1], matrix_out[2], matrix_out[3] = value, value_flow, flow, flow_flow
    base_out[0], base_out[1] = load, load_flow


def prepare(after, *fields):
    height = fields[0].shape[0] // 8
    return pl.pallas_call(
        prepare_kernel,
        out_shape=(tile(height, 2), tile(4), tile(2)),
        in_specs=[ANY] + [VMEM] * 5,
        out_specs=(VMEM,) * 3,
        compiler_params=params(16),
    )(after, *fields)


def source_at(where_ref, sums_ref, h):
    band = h // 16
    sender = (h + band + where_ref[0]) & 15
    return sums_ref[sender * 8 + band]


def load_kernel(where_ref, flag_ref, sums_ref, base_ref, weight_ref, port_out):
    height = weight_ref.shape[0]

    def body(group, carry):
        totals = list(carry)
        for sub in range(8):
            h = group * 8 + sub
            source = source_at(where_ref, sums_ref, h)
            for i in range(2):
                at = i * 4 + sub % 4
                totals[at] = totals[at] + weight_ref[h, i] * source
        return tuple(totals)

    zero = jnp.zeros((8, 128), F32)
    totals = (zero,) * 8
    for group in range(height // 8):
        totals = body(group, totals)
    for i in range(2):
        a, b, c, d = totals[4 * i : 4 * i + 4]
        port_out[i] = base_ref[i] - ((a + b) + (c + d))
    port_out[2] = flag_ref[0]


def load_blocks(where, flag, sums, base, weight):
    return pl.pallas_call(
        load_kernel,
        out_shape=tile(3),
        in_specs=[SMEM] + [VMEM] * 4,
        out_specs=VMEM,
        compiler_params=params(8),
    )(where, flag, sums, base, weight)


def slot_of(me, block):
    steps = (lax.shift_right_logical(block, 1) - lax.shift_right_logical(me, 1)) & 3
    other = (me ^ block) & 1
    odd = jnp.where(lax.shift_right_logical(steps, 1) == (me & 1), 2 + other, 6 - other)
    even = jnp.where(steps == 0, other, 4 + 3 * other)
    return jnp.where((steps & 1) == 1, odd, even)


def block_ends(where_ref, port_of):
    me = where_ref[1]
    zero = jnp.zeros((8, 128), F32)
    drop, level = zero, zero
    draw, feed = zero, zero
    for step in range(8):
        low = jnp.int32(step)
        a, b, c, d, p, j = port_of(slot_of(me, low))
        scale = 1.0 / (c * drop + d)
        new_drop = (a * drop + b) * scale
        new_level = level * scale + (p - new_drop * j)
        below = low < me
        drop, level = jnp.where(below, new_drop, drop), jnp.where(below, new_level, level)
        high = jnp.int32(7 - step)
        a, b, c, d, p, j = port_of(slot_of(me, high))
        scale = 1.0 / (d + draw * b)
        new_draw = (c + draw * a) * scale
        new_feed = (feed - draw * p - j) * scale
        above = high >= me
        draw, feed = jnp.where(above, new_draw, draw), jnp.where(above, new_feed, feed)
    value = (level + drop * feed) / (1.0 + drop * draw)
    return value, feed - draw * value


def middle_kernel(
    after_ref, where_ref, sums_ref, flux_ref, temp_ref, opacity_ref, cond_ref, inertia_ref, kept_out
):
    height = kept_out.shape[0]

    def body(group, carry):
        one, one_flow, two, two_flow, load, load_flow = carry
        for sub in range(8):
            h = group * 8 + sub
            at = pl.ds(group * 64 + sub, 8, stride=8)
            flux, before = flux_ref[at, :], temp_ref[at, :]
            opacity, inertia = opacity_ref[at, :], inertia_ref[at, :]
            face = 1.0 / cond_ref[at, :]
            source = source_at(where_ref, sums_ref, h)
            loss, base, share, emit, rate = first_balance(flux, before, opacity, inertia)
            one, two, load = one + face * one_flow, two + face * two_flow, load + face * load_flow
            kept = (
                one, two, load, face, opacity, inertia, opacity * rate,
                before + (source - emit) * rate, inertia * before + source, 2.0 * flux,
            )
            for i, item in enumerate(kept):
                kept_out[h, i] = item
            one_flow, two_flow = one_flow + loss * one, two_flow + loss * two
            load_flow = load_flow + (loss * load - (base + share * source))
        return one, one_flow, two, two_flow, load, load_flow

    zero = jnp.zeros((8, 128), F32)
    carry = (zero + 1.0, zero, zero, zero + 1.0, zero, zero)
    for group in range(height // 8):
        carry = body(group, carry)


def middle(after, where, sums, *fields):
    height = fields[0].shape[0] // 8
    return pl.pallas_call(
        middle_kernel,
        out_shape=tile(height, 10),
        in_specs=[ANY, SMEM] + [VMEM] * 6,
        out_specs=VMEM,
        compiler_params=params(16),
    )(after, where, sums, *fields)


def second_kernel(where_ref, matrix_ref, loads_ref, middle_ref, kept_out, port_out):
    height = kept_out.shape[0]

    def port_of(at):
        return tuple(matrix_ref[at * 4 + i] for i in range(4)) + tuple(
            loads_ref[at * 3 + i] for i in range(2)
        )

    value, flow = block_ends(where_ref, port_of)

    def body(group, carry):
        one, one_flow, two, two_flow, load, load_flow = carry
        for sub in range(8):
            h = group * 8 + sub
            face, opacity, inertia = middle_ref[h, 3], middle_ref[h, 4], middle_ref[h, 5]
            light = middle_ref[h, 0] * value + middle_ref[h, 1] * flow + middle_ref[h, 2]
            temp = middle_ref[h, 7] + middle_ref[h, 6] * light
            stiff = 16.0 * opacity * (temp * temp * temp)
            emit = 0.25 * stiff * temp
            rate = 1.0 / (inertia + stiff)
            loss = 2.0 + opacity * inertia * rate
            lag = inertia * temp - middle_ref[h, 8]
            right = middle_ref[h, 9] + (emit * inertia - stiff * lag) * rate
            one, two, load = one + face * one_flow, two + face * two_flow, load + face * load_flow
            kept = (one, two, load, opacity * rate, temp - (lag + emit) * rate)
            for i, item in enumerate(kept):
                kept_out[h, i] = item
            one_flow, two_flow = one_flow + loss * one, two_flow + loss * two
            load_flow = load_flow + (loss * load - right)
        return one, one_flow, two, two_flow, load, load_flow

    zero = jnp.zeros((8, 128), F32)
    carry = (zero + 1.0, zero, zero, zero + 1.0, zero, zero)
    for group in range(height // 8):
        carry = body(group, carry)
    one, one_flow, two, two_flow, load, load_flow = carry
    port_out[0], port_out[1], port_out[2], port_out[3] = one, two, one_flow, two_flow
    port_out[4], port_out[5] = load, load_flow


def second_step(where, matrix, loads, kept):
    height = kept.shape[0]
    return pl.pallas_call(
        second_kernel,
        out_shape=(tile(height, 5), tile(6)),
        in_specs=[SMEM] + [VMEM] * 3,
        out_specs=(VMEM, VMEM),
        compiler_params=params(16),
    )(where, matrix, loads, kept)


def finish_kernel(
    where_ref, loads_ref, ports_ref, kept_ref, flux_hbm, temp_hbm, crowded_out, flux_ref, temp_ref, sems
):
    height = kept_ref.shape[0]
    flag = loads_ref[2]
    for block in range(1, 8):
        flag = jnp.maximum(flag, loads_ref[block * 3 + 2])
    crowded_out[0] = jnp.where(jnp.max(flag) > 0.5, 1, 0)

    def port_of(at):
        return tuple(ports_ref[at * 6 + i] for i in range(6))

    value, flow = block_ends(where_ref, port_of)

    def body(group):
        for sub in range(8):
            h = group * 8 + sub
            at = pl.ds(group * 64 + sub, 8, stride=8)
            light = kept_ref[h, 0] * value + kept_ref[h, 1] * flow + kept_ref[h, 2]
            flux_ref[at, :] = light
            temp_ref[at, :] = kept_ref[h, 4] + kept_ref[h, 3] * light

    leaving = [
        pieces(flux_ref, flux_hbm, sems.at[0], PIECE * 8),
        pieces(temp_ref, temp_hbm, sems.at[1], PIECE * 8),
    ]
    for k in range(height // PIECE):
        for group in range(k * PIECE // 8, (k + 1) * PIECE // 8):
            body(group)
        for part in leaving:
            part[k].start()
    for part in leaving:
        for copy in part:
            copy.wait()


def finish(where, loads, ports, kept):
    height = kept.shape[0]
    return pl.pallas_call(
        finish_kernel,
        out_shape=(jax.ShapeDtypeStruct((height * 8, 128), F32),) * 2
        + (jax.ShapeDtypeStruct((1,), jnp.int32),),
        in_specs=[SMEM] + [VMEM] * 3,
        out_specs=(HBM, HBM, SMEM),
        scratch_shapes=[
            pltpu.VMEM((height * 8, 128), F32),
            pltpu.VMEM((height * 8, 128), F32),
            pltpu.SemaphoreType.DMA((2, height // PIECE)),
        ],
        compiler_params=params(16),
    )(where, loads, ports, kept)


def chip_rows(rows):
    return jnp.concatenate([rows, lax.ppermute(rows, "gz", [(i, i ^ 1) for i in range(8)])], 0)


def spread(rows, both):
    across = lax.ppermute(rows, "gz", [(i, (i + 4) % 8) for i in range(8)])
    beside = lax.ppermute(both, "gz", [(i, (i - 2 + 4 * (i % 2)) % 8) for i in range(8)])
    fetched = jnp.concatenate([beside, across], 0)
    passed = lax.ppermute(fetched, "gz", [(i, i ^ 1) for i in range(8)])
    return jnp.concatenate([both, fetched, passed], 0)


def gathered(rows):
    return spread(rows, chip_rows(rows))


def tiles_of(field):
    height, width = field.shape
    return field.reshape(height // 8, 8, width // 128, 128).transpose(0, 2, 1, 3).reshape(-1, 128)


def field_of(tiles, height, width):
    return tiles.reshape(height // 8, width // 128, 8, 128).transpose(0, 2, 1, 3).reshape(height, width)


def shards(
    photon_flux_entering,
    thermal_state_prior,
    opacity_coefficient,
    conductance_scaled,
    thermal_inertia,
    granule_power,
    granule_holder,
    granule_slot,
):
    height, width = photon_flux_entering.shape
    arguments = (
        photon_flux_entering,
        thermal_state_prior,
        opacity_coefficient,
        conductance_scaled,
        thermal_inertia,
        granule_power,
        granule_holder,
        granule_slot,
    )
    where = jnp.stack([lax.axis_index("col"), lax.axis_index("gz")]).astype(jnp.int32)
    sent = pack(granule_holder.reshape(16, 128), granule_slot.reshape(16, 128), granule_power[0])
    got = lax.all_to_all(sent.reshape(16, SLOTS, 128), "col", 0, 0, tiled=True)
    fields = [tiles_of(x) for x in arguments[:5]]
    weight, matrix, base = prepare(sent, *fields)
    matrix = gathered(matrix)
    sums, flag = sum_records(matrix, got.reshape(16 * SLOTS, 128))
    sums = lax.all_to_all(sums.reshape(16, 64, 128), "col", 0, 0, tiled=True).reshape(128, 8, 128)
    loads = load_blocks(where, flag, sums, base, weight)
    both = chip_rows(loads)
    cells = middle(both, where, sums, *fields)
    loads = spread(loads, both)
    kept, ports = second_step(where, matrix, loads, cells)
    flux, temp, crowded = finish(where, loads, gathered(ports), kept)

    def again(state):
        return general_path(*arguments) + (jnp.zeros_like(state[2]),)

    flux, temp = field_of(flux, height, width), field_of(temp, height, width)
    return lax.while_loop(lambda state: state[2][0] > 0, again, (flux, temp, crowded))[:2]


def solution(mesh):
    return jax.shard_map(
        shards,
        mesh=mesh,
        in_specs=(
            P("gz", "col"),
            P("gz", "col"),
            P("gz", "col"),
            P("gz", "col"),
            P("gz", "col"),
            P("gz", "col", None),
            P("gz", "col", None),
            P("gz", "col"),
        ),
        out_specs=(P("gz", "col"), P("gz", "col")),
        check_vma=False,
    )
```

```python
import jax
import jax.numpy as jnp
from jax import lax
from jax.experimental import pallas as pl
from jax.experimental.pallas import tpu as pltpu
from jax.sharding import PartitionSpec as P

NEWTON = 2


radiative_inertia = 2.0


def passed_along(array, axis, by):
    size = lax.axis_size(axis)
    pairs = [(i, i + by) for i in range(size) if 0 <= i + by < size]
    return lax.ppermute(array, axis, pairs)


def padded_2(cells, sides, width):
    for axis, dim in sides:
        count = lax.axis_size(axis)
        ends = count - 1
        head = lax.slice_in_dim(cells, 0, width, axis=dim)
        tail = lax.slice_in_dim(cells, cells.shape[dim] - width, cells.shape[dim], axis=dim)
        cells = jnp.concatenate(
            [
                lax.ppermute(tail, axis, [(i, (i + 1) % count) for i in range(ends)]),
                cells,
                lax.ppermute(head, axis, [((i + 1) % count, i) for i in range(ends)]),
            ],
            axis=dim,
        )
    return cells


def from_below(values, stride):
    filler = jnp.zeros(values.shape[:-2] + (stride,) + values.shape[-1:], values.dtype)
    return jnp.concatenate([filler, values[..., :-stride, :]], -2)


def from_above(values, stride):
    filler = jnp.zeros(values.shape[:-2] + (stride,) + values.shape[-1:], values.dtype)
    return jnp.concatenate([values[..., stride:, :], filler], -2)


def combine_rows(
    lower_ratio,
    upper_ratio,
    scaled_rhs,
    lower_below,
    upper_below,
    rhs_below,
    lower_above,
    upper_above,
    rhs_above,
):
    pivot = 1.0 - lower_ratio * upper_below - upper_ratio * lower_above
    new_rhs = (scaled_rhs - lower_ratio * rhs_below - upper_ratio * rhs_above) / pivot
    return (-lower_ratio * lower_below / pivot, -upper_ratio * upper_above / pivot, new_rhs)


def reduce_block(lower_ratio, upper_ratio, scaled_rhs):
    height = lower_ratio.shape[0]
    stride = 1
    while stride < height:
        lower_ratio, upper_ratio, scaled_rhs = combine_rows(
            lower_ratio,
            upper_ratio,
            scaled_rhs,
            from_below(lower_ratio, stride),
            from_below(upper_ratio, stride),
            from_below(scaled_rhs, stride),
            from_above(lower_ratio, stride),
            from_above(upper_ratio, stride),
            from_above(scaled_rhs, stride),
        )
        stride = stride * 2
    return scaled_rhs


def chain_levels(stacked):
    count = lax.axis_size("gz")
    stride = 1
    while stride < count:
        below = passed_along(stacked, "gz", stride)
        above = passed_along(stacked, "gz", -stride)
        stacked = jnp.stack(
            combine_rows(
                stacked[0],
                stacked[1],
                stacked[2],
                below[0],
                below[1],
                below[2],
                above[0],
                above[1],
                above[2],
            )
        )
        stride = stride * 2
    return stacked[2]


def gather_sources(granule_power, granule_holder, granule_slot, cell_rows):
    heat = granule_power[0]
    owners = granule_holder[0, :, 0]
    cells = granule_slot[0]
    total = jnp.zeros((cell_rows, 128), jnp.float32)
    n_owner = lax.axis_size("col")
    capacity_slots = 4 * heat.shape[0] // n_owner
    member = (owners[:, None] == jnp.arange(n_owner, dtype=jnp.int32)[None, :]).astype(jnp.int32)
    slots = jnp.sum((jnp.cumsum(member, 0) - 1) * member, 1)
    send_heat = jnp.zeros((n_owner, capacity_slots, 128), jnp.float32).at[owners, slots].set(heat)
    send_cell = (
        jnp.zeros((n_owner, capacity_slots), jnp.float32)
        .at[owners, slots]
        .set(cells.astype(jnp.float32))
    )
    got_heat, got_cell = (
        lax.all_to_all(send_heat, "col", split_axis=0, concat_axis=0, tiled=True),
        lax.all_to_all(send_cell, "col", split_axis=0, concat_axis=0, tiled=True),
    )
    return total.at[got_cell.reshape(-1).astype(jnp.int32)].add(got_heat.reshape(-1, 128))


def general_path(
    photon_flux_entering,
    thermal_state_prior,
    opacity_coefficient,
    conductance_scaled,
    thermal_inertia,
    granule_power,
    granule_holder,
    granule_slot,
):
    height, width = photon_flux_entering.shape
    seg_count = width // 128
    deposited_power = gather_sources(
        granule_power, granule_holder, granule_slot, height * seg_count
    ).reshape(height, width)
    edge = passed_along(conductance_scaled[:1], "gz", -1)
    diff_up = jnp.concatenate([conductance_scaled[1:], edge], 0)
    places = lax.broadcasted_iota(jnp.int32, (height, 1), 0)
    has_below = (lax.axis_index("gz") > 0).astype(jnp.float32)
    subdiagonal_entries = -conductance_scaled * jnp.where(places == 0, has_below, 1.0)
    superdiagonal_entries = -diff_up
    photon_flux_final, thermal_state_final = (photon_flux_entering, thermal_state_prior)
    for step in range(NEWTON):
        coupling_weight = 16.0 * opacity_coefficient * thermal_state_final**3
        blackbody_output = 4.0 * opacity_coefficient * thermal_state_final**4
        padded = padded_2(photon_flux_final, (("gz", 0),), 1)
        below, above = (padded[:-2], padded[2:])
        flux_mismatch = (
            conductance_scaled * (photon_flux_final - below)
            + diff_up * (photon_flux_final - above)
            + radiative_inertia * (photon_flux_final - photon_flux_entering)
            + opacity_coefficient * photon_flux_final
            - blackbody_output
        )
        thermal_mismatch = (
            thermal_inertia * (thermal_state_final - thermal_state_prior)
            + blackbody_output
            - opacity_coefficient * photon_flux_final
            - deposited_power
        )
        jacobian_divisor = thermal_inertia + coupling_weight
        forcing_vector = -flux_mismatch - coupling_weight * thermal_mismatch / jacobian_divisor
        main_band_entries = (
            conductance_scaled
            + diff_up
            + radiative_inertia
            + opacity_coefficient * thermal_inertia / jacobian_divisor
        )
        lower_ratio = subdiagonal_entries / main_band_entries
        upper_ratio = superdiagonal_entries / main_band_entries
        closed_lower = jnp.where((places == 0) | (places == height - 1), 0.0, lower_ratio)
        closed_upper = jnp.where(places >= height - 2, 0.0, upper_ratio)
        right_sides = jnp.stack(
            [
                jnp.where(places == height - 1, 0.0, forcing_vector / main_band_entries),
                jnp.where(places == 0, -lower_ratio, 0.0),
                jnp.where(places == height - 2, -upper_ratio, 0.0)
                + jnp.where(places == height - 1, 1.0, 0.0),
            ]
        )
        local = reduce_block(closed_lower, closed_upper, right_sides)
        nearby = passed_along(local[:, 0, :], "gz", -1)
        top_lower = subdiagonal_entries[-1]
        top_upper = superdiagonal_entries[-1]
        alpha = top_lower * local[1, -2]
        beta = main_band_entries[-1] + top_lower * local[2, -2] + top_upper * nearby[1]
        gamma = top_upper * nearby[2]
        value = forcing_vector[-1] - top_lower * local[0, -2] - top_upper * nearby[0]
        stacked = jnp.stack([alpha / beta, gamma / beta, value / beta])
        interface = chain_levels(stacked)
        lower_value = passed_along(interface, "gz", 1)
        thermal_increment = (
            local[0] + local[1] * lower_value[None, :] + local[2] * interface[None, :]
        )
        photon_flux_final = photon_flux_final + thermal_increment
        thermal_state_final = (
            thermal_state_final
            + (opacity_coefficient * thermal_increment - thermal_mismatch) / jacobian_divisor
        )
    return (photon_flux_final, thermal_state_final)


SLOTS = 192
ROOM = 190
PIECE = 16
F32 = jnp.float32
BF16 = jnp.bfloat16
VMEM = pl.BlockSpec(memory_space=pltpu.VMEM)
SMEM = pl.BlockSpec(memory_space=pltpu.SMEM)
ANY = pl.BlockSpec(memory_space=pl.ANY)
HBM = pl.BlockSpec(memory_space=pltpu.HBM)


def params(mib):
    return pltpu.CompilerParams(vmem_limit_bytes=mib * 2**20)


def tile(*count):
    return jax.ShapeDtypeStruct(count + (8, 128), F32)


def pieces(source, sink, sems, rows):
    return [
        pltpu.make_async_copy(
            source.at[pl.ds(k * rows, rows)], sink.at[pl.ds(k * rows, rows)], sems.at[k]
        )
        for k in range(source.shape[0] // rows)
    ]


def pack_kernel(owner_ref, cell_ref, heat_hbm, out_ref, heat_ref, row_vmem, row_smem, sem, heat_sem):
    heat_copy = pltpu.make_async_copy(heat_hbm, heat_ref, heat_sem)
    heat_copy.start()
    groups, lanes = owner_ref.shape
    owner, cell = owner_ref[...], cell_ref[...]
    level = lax.shift_right_logical(cell, 3)
    band = lax.shift_right_logical(level, 4)
    target = (level + band + owner) & 15
    place = owner * 64 + band * 8 + (cell & 7) + 1
    place_high = lax.shift_right_logical(place, 5).astype(F32)
    place_low = (place & 31).astype(F32)
    classes = lax.broadcasted_iota(jnp.int32, (16, lanes), 0)
    member = [jnp.where(classes == target[g : g + 1, :], 1.0, 0.0) for g in range(groups)]
    source = lax.broadcasted_iota(jnp.int32, (lanes, 2 * lanes), 0)
    sink = lax.broadcasted_iota(jnp.int32, (lanes, 2 * lanes), 1)
    before = jnp.where((source < sink) | (sink >= lanes), 1.0, 0.0).astype(BF16)
    counts = jnp.dot(jnp.concatenate(member, 0).astype(BF16), before, preferred_element_type=F32)
    start = jnp.zeros((16, lanes), F32)
    slots = []
    for g in range(groups):
        ahead = counts[16 * g : 16 * g + 16]
        slots.append(jnp.sum(member[g] * (ahead[:, :lanes] + start), 0, keepdims=True))
        start = start + ahead[:, lanes:]
    slot = jnp.concatenate(slots, 0).astype(jnp.int32)
    fits = slot < ROOM
    row_vmem[...] = target * SLOTS + jnp.where(fits, slot, SLOTS - 1)
    copy = pltpu.make_async_copy(row_vmem, row_smem, sem)
    copy.start()
    out_ref[...] = jnp.zeros_like(out_ref)
    named = jnp.where(fits, slot, 4096)
    slot_row = lax.broadcasted_iota(jnp.int32, (2 * lanes, lanes), 0)
    weights = jnp.concatenate(
        [
            jnp.concatenate([member[g] * part[g : g + 1] for g in range(groups)], 1)
            for part in (place_high, place_low)
        ],
        0,
    ).astype(BF16)
    hits = jnp.concatenate(
        [jnp.where(slot_row == named[g : g + 1], 1.0, 0.0).astype(BF16) for g in range(groups)], 1
    )
    table = lax.dot_general(weights, hits, (((1,), (1,)), ((), ())), preferred_element_type=F32)
    places = table[:16] * 32.0 + table[16:] - 1.0
    over = jnp.max(jnp.where(start > ROOM, 1.0, 0.0))
    lane = lax.broadcasted_iota(jnp.int32, (1, 2 * lanes), 1)
    places = jnp.where(lane == 2 * lanes - 1, over, places)
    copy.wait()
    heat_copy.wait()

    for g in range(groups):
        for i in range(lanes):
            row = row_smem[g, i]
            out_ref[pl.ds(row, 1), :] = heat_ref[g * lanes + i : g * lanes + i + 1, :]

    for m in range(16):
        out_ref[m * SLOTS + ROOM : m * SLOTS + ROOM + 1, :] = places[m : m + 1, :lanes]
        out_ref[m * SLOTS + ROOM + 1 : m * SLOTS + SLOTS, :] = places[m : m + 1, lanes:]


def pack(owner, cell, heat):
    return pl.pallas_call(
        pack_kernel,
        out_shape=jax.ShapeDtypeStruct((16 * SLOTS, 128), F32),
        in_specs=[VMEM, VMEM, HBM],
        out_specs=VMEM,
        scratch_shapes=[
            pltpu.VMEM((2048, 128), F32),
            pltpu.VMEM((16, 128), jnp.int32),
            pltpu.SMEM((16, 128), jnp.int32),
            pltpu.SemaphoreType.DMA,
            pltpu.SemaphoreType.DMA,
        ],
        compiler_params=params(16),
    )(owner, cell, heat)


def sum_kernel(after_ref, got_ref, out_hbm, flag_ref, terms, out_ref, sems):
    flag = jnp.zeros((1, 128), F32)
    for s in range(16):
        heat = got_ref[s * SLOTS : (s + 1) * SLOTS, :]
        high = heat.astype(BF16)
        terms[s * SLOTS : (s + 1) * SLOTS, :128] = high
        terms[s * SLOTS : (s + 1) * SLOTS, 128:] = (heat - high.astype(F32)).astype(BF16)
        flag = jnp.maximum(flag, got_ref[(s + 1) * SLOTS - 1 : (s + 1) * SLOTS, :])
    lane = lax.broadcasted_iota(jnp.int32, (1, 128), 1)
    flag = jnp.where(lane == 127, flag, 0.0)
    flag_ref[0] = jnp.broadcast_to(flag, (8, 128))
    left = lane < 64
    names = []
    for s in range(0, 16, 2):
        rows = [
            got_ref[at : at + 1, :]
            for block in (s, s + 1)
            for at in (block * SLOTS + ROOM, block * SLOTS + ROOM + 1)
        ]
        turned = pltpu.roll(rows[2], 64, 1)
        names += [
            rows[0],
            jnp.where(left, rows[1], turned),
            jnp.where(left, turned, pltpu.roll(rows[3], 64, 1)),
        ]
    names = jnp.concatenate(names, 1)
    row = lax.broadcasted_iota(jnp.int32, (128, 128), 0).astype(F32).astype(BF16)
    leaving = pieces(out_ref, out_hbm, sems, 128)

    for block in range(8):
        near = (names - block * 128.0).astype(BF16)
        hits = [
            jnp.where(row == near[:, g * 128 : (g + 1) * 128], BF16(1.0), BF16(0.0)) for g in range(24)
        ]
        both = jnp.dot(jnp.concatenate(hits, 1), terms[...], preferred_element_type=F32)
        out_ref[block * 128 : (block + 1) * 128, :] = both[:, :128] + both[:, 128:]
        leaving[block].start()
    for copy in leaving:
        copy.wait()


def sum_records(after, got):
    return pl.pallas_call(
        sum_kernel,
        out_shape=(jax.ShapeDtypeStruct((1024, 128), F32), tile(1)),
        in_specs=[ANY, VMEM],
        out_specs=(HBM, VMEM),
        scratch_shapes=[
            pltpu.VMEM((16 * SLOTS, 256), BF16),
            pltpu.VMEM((1024, 128), F32),
            pltpu.SemaphoreType.DMA((8,)),
        ],
        compiler_params=params(24),
    )(after, got)


def first_balance(flux, temp, opacity, inertia):
    stiff = 16.0 * opacity * (temp * temp * temp)
    emit = 0.25 * stiff * temp
    rate = 1.0 / (inertia + stiff)
    loss = 2.0 + opacity * inertia * rate
    return loss, 2.0 * flux + emit * inertia * rate, stiff * rate, emit, rate


def prepare_kernel(
    after_ref, flux_ref, temp_ref, opacity_ref, cond_ref, inertia_ref, weight_out, matrix_out, base_out
):
    height = weight_out.shape[0]

    def body(step, carry):
        value, value_flow, flow, flow_flow, load, load_flow = carry
        for sub in range(8):
            group = height // 8 - 1 - step
            h = group * 8 + 7 - sub
            at = pl.ds(group * 64 + 7 - sub, 8, stride=8)
            loss, base, share, _, _ = first_balance(
                flux_ref[at, :], temp_ref[at, :], opacity_ref[at, :], inertia_ref[at, :]
            )
            face = 1.0 / cond_ref[at, :]
            weight_out[h, 0], weight_out[h, 1] = value_flow * share, flow_flow * share
            load, load_flow = load - value_flow * base, load_flow - flow_flow * base
            value, flow = value + loss * value_flow, flow + loss * flow_flow
            value_flow, flow_flow = value_flow + face * value, flow_flow + face * flow
        return value, value_flow, flow, flow_flow, load, load_flow

    zero = jnp.zeros((8, 128), F32)
    value, value_flow, flow, flow_flow, load, load_flow = lax.fori_loop(
        0, height // 8, body, (zero + 1.0, zero, zero, zero + 1.0, zero, zero)
    )
    matrix_out[0], matrix_out[1], matrix_out[2], matrix_out[3] = value, value_flow, flow, flow_flow
    base_out[0], base_out[1] = load, load_flow


def prepare(after, *fields):
    height = fields[0].shape[0] // 8
    return pl.pallas_call(
        prepare_kernel,
        out_shape=(tile(height, 2), tile(4), tile(2)),
        in_specs=[ANY] + [VMEM] * 5,
        out_specs=(VMEM,) * 3,
        compiler_params=params(16),
    )(after, *fields)


def source_at(where_ref, sums_ref, h):
    band = h // 16
    sender = (h + band + where_ref[0]) & 15
    return sums_ref[sender * 8 + band]


def load_kernel(where_ref, flag_ref, sums_ref, base_ref, weight_ref, port_out):
    height = weight_ref.shape[0]

    def body(group, carry):
        totals = list(carry)
        for sub in range(8):
            h = group * 8 + sub
            source = source_at(where_ref, sums_ref, h)
            for i in range(2):
                at = i * 4 + sub % 4
                totals[at] = totals[at] + weight_ref[h, i] * source
        return tuple(totals)

    zero = jnp.zeros((8, 128), F32)
    totals = (zero,) * 8
    for group in range(height // 8):
        totals = body(group, totals)
    for i in range(2):
        a, b, c, d = totals[4 * i : 4 * i + 4]
        port_out[i] = base_ref[i] - ((a + b) + (c + d))
    port_out[2] = flag_ref[0]


def load_blocks(where, flag, sums, base, weight):
    return pl.pallas_call(
        load_kernel,
        out_shape=tile(3),
        in_specs=[SMEM] + [VMEM] * 4,
        out_specs=VMEM,
        compiler_params=params(8),
    )(where, flag, sums, base, weight)


def slot_of(me, block):
    steps = (lax.shift_right_logical(block, 1) - lax.shift_right_logical(me, 1)) & 3
    other = (me ^ block) & 1
    odd = jnp.where(lax.shift_right_logical(steps, 1) == (me & 1), 2 + other, 6 - other)
    even = jnp.where(steps == 0, other, 4 + 3 * other)
    return jnp.where((steps & 1) == 1, odd, even)


def block_ends(where_ref, port_of):
    me = where_ref[1]
    zero = jnp.zeros((8, 128), F32)
    drop, level = zero, zero
    draw, feed = zero, zero
    for step in range(8):
        low = jnp.int32(step)
        a, b, c, d, p, j = port_of(slot_of(me, low))
        scale = 1.0 / (c * drop + d)
        new_drop = (a * drop + b) * scale
        new_level = level * scale + (p - new_drop * j)
        below = low < me
        drop, level = jnp.where(below, new_drop, drop), jnp.where(below, new_level, level)
        high = jnp.int32(7 - step)
        a, b, c, d, p, j = port_of(slot_of(me, high))
        scale = 1.0 / (d + draw * b)
        new_draw = (c + draw * a) * scale
        new_feed = (feed - draw * p - j) * scale
        above = high >= me
        draw, feed = jnp.where(above, new_draw, draw), jnp.where(above, new_feed, feed)
    value = (level + drop * feed) / (1.0 + drop * draw)
    return value, feed - draw * value


def middle_kernel(
    after_ref, where_ref, sums_ref, flux_ref, temp_ref, opacity_ref, cond_ref, inertia_ref, kept_out
):
    height = kept_out.shape[0]

    def body(group, carry):
        one, one_flow, two, two_flow, load, load_flow = carry
        for sub in range(8):
            h = group * 8 + sub
            at = pl.ds(group * 64 + sub, 8, stride=8)
            flux, before = flux_ref[at, :], temp_ref[at, :]
            opacity, inertia = opacity_ref[at, :], inertia_ref[at, :]
            face = 1.0 / cond_ref[at, :]
            source = source_at(where_ref, sums_ref, h)
            loss, base, share, emit, rate = first_balance(flux, before, opacity, inertia)
            one, two, load = one + face * one_flow, two + face * two_flow, load + face * load_flow
            kept = (
                one, two, load, face, opacity, inertia, opacity * rate,
                before + (source - emit) * rate, inertia * before + source, 2.0 * flux,
            )
            for i, item in enumerate(kept):
                kept_out[h, i] = item
            one_flow, two_flow = one_flow + loss * one, two_flow + loss * two
            load_flow = load_flow + (loss * load - (base + share * source))
        return one, one_flow, two, two_flow, load, load_flow

    zero = jnp.zeros((8, 128), F32)
    carry = (zero + 1.0, zero, zero, zero + 1.0, zero, zero)
    for group in range(height // 8):
        carry = body(group, carry)


def middle(after, where, sums, *fields):
    height = fields[0].shape[0] // 8
    return pl.pallas_call(
        middle_kernel,
        out_shape=tile(height, 10),
        in_specs=[ANY, SMEM] + [VMEM] * 6,
        out_specs=VMEM,
        compiler_params=params(16),
    )(after, where, sums, *fields)


def second_kernel(where_ref, matrix_ref, loads_ref, middle_ref, kept_out, port_out):
    height = kept_out.shape[0]

    def port_of(at):
        return tuple(matrix_ref[at * 4 + i] for i in range(4)) + tuple(
            loads_ref[at * 3 + i] for i in range(2)
        )

    value, flow = block_ends(where_ref, port_of)

    def body(group, carry):
        one, one_flow, two, two_flow, load, load_flow = carry
        for sub in range(8):
            h = group * 8 + sub
            face, opacity, inertia = middle_ref[h, 3], middle_ref[h, 4], middle_ref[h, 5]
            light = middle_ref[h, 0] * value + middle_ref[h, 1] * flow + middle_ref[h, 2]
            temp = middle_ref[h, 7] + middle_ref[h, 6] * light
            stiff = 16.0 * opacity * (temp * temp * temp)
            emit = 0.25 * stiff * temp
            rate = 1.0 / (inertia + stiff)
            loss = 2.0 + opacity * inertia * rate
            lag = inertia * temp - middle_ref[h, 8]
            right = middle_ref[h, 9] + (emit * inertia - stiff * lag) * rate
            one, two, load = one + face * one_flow, two + face * two_flow, load + face * load_flow
            kept = (one, two, load, opacity * rate, temp - (lag + emit) * rate)
            for i, item in enumerate(kept):
                kept_out[h, i] = item
            one_flow, two_flow = one_flow + loss * one, two_flow + loss * two
            load_flow = load_flow + (loss * load - right)
        return one, one_flow, two, two_flow, load, load_flow

    zero = jnp.zeros((8, 128), F32)
    carry = (zero + 1.0, zero, zero, zero + 1.0, zero, zero)
    for group in range(height // 8):
        carry = body(group, carry)
    one, one_flow, two, two_flow, load, load_flow = carry
    port_out[0], port_out[1], port_out[2], port_out[3] = one, two, one_flow, two_flow
    port_out[4], port_out[5] = load, load_flow


def second_step(where, matrix, loads, kept):
    height = kept.shape[0]
    return pl.pallas_call(
        second_kernel,
        out_shape=(tile(height, 5), tile(6)),
        in_specs=[SMEM] + [VMEM] * 3,
        out_specs=(VMEM, VMEM),
        compiler_params=params(16),
    )(where, matrix, loads, kept)


def finish_kernel(
    where_ref, loads_ref, ports_ref, kept_ref, flux_hbm, temp_hbm, crowded_out, flux_ref, temp_ref, sems
):
    height = kept_ref.shape[0]
    flag = loads_ref[2]
    for block in range(1, 8):
        flag = jnp.maximum(flag, loads_ref[block * 3 + 2])
    crowded_out[0] = jnp.where(jnp.max(flag) > 0.5, 1, 0)

    def port_of(at):
        return tuple(ports_ref[at * 6 + i] for i in range(6))

    value, flow = block_ends(where_ref, port_of)

    def body(group):
        for sub in range(8):
            h = group * 8 + sub
            at = pl.ds(group * 64 + sub, 8, stride=8)
            light = kept_ref[h, 0] * value + kept_ref[h, 1] * flow + kept_ref[h, 2]
            flux_ref[at, :] = light
            temp_ref[at, :] = kept_ref[h, 4] + kept_ref[h, 3] * light

    leaving = [
        pieces(flux_ref, flux_hbm, sems.at[0], PIECE * 8),
        pieces(temp_ref, temp_hbm, sems.at[1], PIECE * 8),
    ]
    for k in range(height // PIECE):
        for group in range(k * PIECE // 8, (k + 1) * PIECE // 8):
            body(group)
        for part in leaving:
            part[k].start()
    for part in leaving:
        for copy in part:
            copy.wait()


def finish(where, loads, ports, kept):
    height = kept.shape[0]
    return pl.pallas_call(
        finish_kernel,
        out_shape=(jax.ShapeDtypeStruct((height * 8, 128), F32),) * 2
        + (jax.ShapeDtypeStruct((1,), jnp.int32),),
        in_specs=[SMEM] + [VMEM] * 3,
        out_specs=(HBM, HBM, SMEM),
        scratch_shapes=[
            pltpu.VMEM((height * 8, 128), F32),
            pltpu.VMEM((height * 8, 128), F32),
            pltpu.SemaphoreType.DMA((2, height // PIECE)),
        ],
        compiler_params=params(16),
    )(where, loads, ports, kept)


def chip_rows(rows):
    return jnp.concatenate([rows, lax.ppermute(rows, "gz", [(i, i ^ 1) for i in range(8)])], 0)


def spread(rows, both):
    across = lax.ppermute(rows, "gz", [(i, (i + 4) % 8) for i in range(8)])
    beside = lax.ppermute(both, "gz", [(i, (i - 2 + 4 * (i % 2)) % 8) for i in range(8)])
    fetched = jnp.concatenate([beside, across], 0)
    passed = lax.ppermute(fetched, "gz", [(i, i ^ 1) for i in range(8)])
    return jnp.concatenate([both, fetched, passed], 0)


def gathered(rows):
    return spread(rows, chip_rows(rows))


def tiles_of(field):
    height, width = field.shape
    return field.reshape(height // 8, 8, width // 128, 128).transpose(0, 2, 1, 3).reshape(-1, 128)


def field_of(tiles, height, width):
    return tiles.reshape(height // 8, width // 128, 8, 128).transpose(0, 2, 1, 3).reshape(height, width)


def shards(
    photon_flux_entering,
    thermal_state_prior,
    opacity_coefficient,
    conductance_scaled,
    thermal_inertia,
    granule_power,
    granule_holder,
    granule_slot,
):
    height, width = photon_flux_entering.shape
    arguments = (
        photon_flux_entering,
        thermal_state_prior,
        opacity_coefficient,
        conductance_scaled,
        thermal_inertia,
        granule_power,
        granule_holder,
        granule_slot,
    )
    where = jnp.stack([lax.axis_index("col"), lax.axis_index("gz")]).astype(jnp.int32)
    sent = pack(granule_holder.reshape(16, 128), granule_slot.reshape(16, 128), granule_power[0])
    got = lax.all_to_all(sent.reshape(16, SLOTS, 128), "col", 0, 0, tiled=True)
    fields = [tiles_of(x) for x in arguments[:5]]
    weight, matrix, base = prepare(sent, *fields)
    matrix = gathered(matrix)
    sums, flag = sum_records(matrix, got.reshape(16 * SLOTS, 128))
    sums = lax.all_to_all(sums.reshape(16, 64, 128), "col", 0, 0, tiled=True).reshape(128, 8, 128)
    loads = load_blocks(where, flag, sums, base, weight)
    both = chip_rows(loads)
    cells = middle(both, where, sums, *fields)
    loads = spread(loads, both)
    kept, ports = second_step(where, matrix, loads, cells)
    flux, temp, crowded = finish(where, loads, gathered(ports), kept)

    def again(state):
        return general_path(*arguments) + (jnp.zeros_like(state[2]),)

    flux, temp = field_of(flux, height, width), field_of(temp, height, width)
    return lax.while_loop(lambda state: state[2] > 0, again, (flux, temp, crowded.reshape(())))[:2]


def solution(mesh):
    return jax.shard_map(
        shards,
        mesh=mesh,
        in_specs=(
            P("gz", "col"),
            P("gz", "col"),
            P("gz", "col"),
            P("gz", "col"),
            P("gz", "col"),
            P("gz", "col", None),
            P("gz", "col", None),
            P("gz", "col"),
        ),
        out_specs=(P("gz", "col"), P("gz", "col")),
        check_vma=False,
    )
```
